32 devices in a mesh: groups: 2 (over y), dp: 4 (over z), expert: 2 (over x), tensor: 2 (over core).
Axes of the slice: x: 2, y: 2, z: 4, core: 2. Of those that a mesh axis runs over, the one named last changes fastest.
Arguments:
- tokens: bfloat16 [2048, 6144], P(('groups', 'dp', 'expert'), 'tensor'), parts along dimension 0, may hold values from -6 to 6
- routes: int32 [2048, 2], P(('groups', 'dp', 'expert')), parts along dimension 0, may hold values from 0 to 3, all different within a row; in each aligned block of 128 rows (0 to 127, 128 to 255, ...) at most 80 rows name the same one
- route_weight: float32 [2048, 2], P(('groups', 'dp', 'expert')), parts along dimension 0, may hold values from 0.2 to 1
- block_tenant: int32 [16], P('groups'), parts along dimension 0, may hold values from 0 to 31
- page_table: int32 [4, 32], replicated, may hold values from 0 to 31, each once within a row
- adapter_in: bfloat16 [4, 32, 32, 6144], P('expert', None, None, ('tensor', 'dp')), may hold values from -0.078125 to 0.078125
- adapter_down: bfloat16 [4, 32, 16, 6144], P('expert', None, None, ('tensor', 'dp')), may hold values from -1.5 to 1.5
- upstream: bfloat16 [2048, 6144], P(('groups', 'dp', 'expert'), 'tensor'), parts along dimension 0, may hold values from -6 to 6
Outputs:
- adapted: bfloat16 [2048, 6144], P(('groups', 'dp', 'expert'), 'tensor'), parts along dimension 0
- grad_tokens: bfloat16 [2048, 6144], P(('groups', 'dp', 'expert'), 'tensor'), parts along dimension 0
- grad_weight: float32 [2048, 2], P(('groups', 'dp', 'expert')), parts along dimension 0
- grad_in: float32 [8, 32, 32, 6144], P(('groups', 'expert'), None, None, ('tensor', 'dp')), parts along dimension 0
- grad_down: float32 [8, 32, 16, 6144], P(('groups', 'expert'), None, None, ('tensor', 'dp')), parts along dimension 0
The draws below stay inside these ranges and needn't reach their ends.
There are 2 independent parts, one for each index of `groups`. The reference program is written for one: setup_inputs(seed, part) draws one part's arguments, and reference() takes and returns one part's arrays. A program takes and returns all parts, laid end to end along the dimension named above; an argument that names none is the same for every part. Nothing has to cross between parts.
Inputs may be any that keep to these rules, and one draw needn't show every extreme that they name: `routes`: the two experts of a token differ; among the 128 tokens of one device no expert is named more than 80 times, and some device names some expert exactly 80 times.
All inputs are finite; a program needn't handle non-finite values.
Results may differ from the reference program's by a relative error of at most 0.0065.
Values may be sent and summed in bfloat16 or wider, within the bound.
A program may use at most 128 MiB of HBM per device.

```python
import math
import jax
import jax.numpy as jnp
import numpy as np
from jax import lax

D = 6144
R = 16
TOP = 2
TENANTS = 32
TOK_DEV = 128
EXPERTS = 4
MOST = 80
BLOCKS = 8
TOKENS = 1024


def place_ends(values, stream_key, smallest, top_value):
    shape = values.shape
    place = [jax.random.randint(jax.random.fold_in(stream_key, axis), (), 0, shape[axis]) for axis in range(len(shape))]
    values = values.at[tuple(place)].set(smallest)
    longest = shape.index(max(shape))
    place[longest] = (place[longest] + 1) % shape[longest]
    return values.at[tuple(place)].set(top_value)


def block_levels(own_key, shape, shards, least, top_value):
    factor_of = 1.0
    for axis_at, blocks in shards:
        draws = jax.random.uniform(jax.random.fold_in(jax.random.fold_in(own_key, 6), axis_at), (blocks,), jnp.float32, least / len(shards), top_value / len(shards))
        factor_of = factor_of * jnp.repeat(jnp.exp(draws), shape[axis_at] // blocks).reshape((-1,) + (1,) * (len(shape) - 1 - axis_at))
    return factor_of


def shared_out(stream_key, own, number, rows, amount, top, bound, skew):
    sequence = jax.random.permutation(stream_key, amount)
    crowded, usual = portions_of(amount, rows * top, bound, skew, True), portions_of(amount, rows * top, bound, skew, False)
    places = jnp.arange(amount)

    def named(sizes, offset_by):
        used = int((sizes > 0).sum())
        fixed = max(1, used // 4)
        moved = fixed + (places - fixed + offset_by * (used - fixed)) % max(1, amount - fixed)
        return jnp.zeros((amount,), jnp.int32).at[sequence[jnp.where(places < fixed, places, moved)]].set(jnp.asarray(sizes, jnp.int32))

    sizes = jnp.where(number % 4 == 0, named(crowded, number // 4), named(usual, number - number // 4 - 1))
    mixed = jax.random.permutation(jax.random.fold_in(own, 3), amount)
    giver, taker = mixed[0:amount // 2 * 2:2], mixed[1:amount // 2 * 2:2]
    room = jnp.minimum(sizes[giver] - 1, bound - sizes[taker]) // 2
    room = jnp.where((giver == sequence[0]) | (taker == sequence[0]) | (sizes[taker] == 0), 0, jnp.maximum(room, 0))
    moved = jax.random.randint(jax.random.fold_in(own, 4), (amount // 2,), 0, 1 << 20) % (room + 1)
    sizes = sizes.at[giver].add(-moved).at[taker].add(moved)
    members = jnp.searchsorted(jnp.cumsum(sizes), jnp.arange(rows * top), side="right").astype(jnp.int32)
    table = members.reshape(top, rows).T
    table = table[jax.random.permutation(jax.random.fold_in(own, 1), rows)]
    offset_by = jax.random.randint(jax.random.fold_in(own, 2), (rows, 1), 0, top)
    return jnp.take_along_axis(table, (jnp.arange(top)[None, :] + offset_by) % top, axis=1)


def portions_of(number_of, total, most, slope, full):
    loads = [(1 << 20) // math.isqrt(standing ** slope) + 1 for standing in range(1, number_of + 1)]
    largest = most if full else min(most, max(-(-total // number_of), total * loads[0] // sum(loads)))
    least = 1 if total - largest >= number_of - 1 else 0
    given, surplus = [largest] + [least] * (number_of - 1), total - largest - least * (number_of - 1)
    while surplus > 0:
        movable = [i for i in range(1, number_of) if given[i] < largest] or [i for i in range(1, number_of) if given[i] < most]
        mass, budget = sum([loads[i] for i in movable]), surplus
        for i in movable:
            extra = min(most - given[i], max(1, budget * loads[i] // mass), surplus)
            given[i] = given[i] + extra
            surplus = surplus - extra
    return np.array(given)


def noise(own_key, dims, scale, bound, split=(), kind=jnp.bfloat16):
    result = jax.random.normal(own_key, dims, jnp.float32) * scale
    if len(split) > 0:
        result = block_levels(own_key, dims, split, -0.22, 0.18) * result
    return jnp.clip(result, min=-bound, max=bound).astype(kind)


def setup_inputs(seed: int = 0, part: int = 0) -> dict:
    seeds = jax.random.split(jax.random.key(seed), 9)
    own_keys = jax.random.split(jax.random.fold_in(seeds[8], part), 9)
    tokens = noise(own_keys[0], (TOKENS, D), 1.0, 6.0, ((0, 8), (1, 2)))
    routes_keys = jax.random.split(jax.random.fold_in(own_keys[1], 1), TOKENS // TOK_DEV)
    routes_turns = jax.random.permutation(jax.random.fold_in(own_keys[1], 3), TOKENS // TOK_DEV)
    routes = jax.vmap(lambda own, number: shared_out(jax.random.fold_in(own_keys[1], 2), own, number, TOK_DEV, EXPERTS, TOP, MOST, 1))(routes_keys, routes_turns).reshape((TOKENS, TOP))
    route_weight = jnp.clip(0.2 + 0.8 * jax.random.uniform(own_keys[2], (TOKENS, TOP), jnp.float32) ** block_levels(own_keys[2], (TOKENS, TOP), ((0, 8),), -0.2, 0.2), 0.2, 1.0)
    block_tenant = place_ends(jax.random.randint(own_keys[3], (BLOCKS,), 0, TENANTS), jax.random.fold_in(own_keys[3], 1), 0, TENANTS - 1).astype(jnp.int32)
    page_table = jax.vmap(lambda own: jax.random.permutation(own, TENANTS))(jax.random.split(seeds[4], EXPERTS)).reshape((EXPERTS, TENANTS)).astype(jnp.int32)
    adapter_in = noise(seeds[5], (EXPERTS, TENANTS, 2 * R, D), D ** -0.5, 0.078125, ((0, 2), (3, 8)))
    adapter_down = noise(seeds[6], (EXPERTS, TENANTS, R, D), R ** -0.5, 1.5, ((0, 2), (3, 8)))
    upstream = noise(own_keys[7], (TOKENS, D), 1.0, 6.0, ((0, 8), (1, 2)))
    return {"tokens": tokens, "routes": routes, "route_weight": route_weight, "block_tenant": block_tenant, "page_table": page_table, "adapter_in": adapter_in, "adapter_down": adapter_down, "upstream": upstream}


def rounded(value):
    return lax.optimization_barrier(value.astype(jnp.bfloat16)).astype(jnp.float32)


def reference(tokens, routes, route_weight, block_tenant, page_table, adapter_in, adapter_down, upstream):
    ids = jnp.arange(EXPERTS, dtype=jnp.int32)

    def step(carry, items):
        grad_in, grad_down = carry
        rows, route, weight, tenant, cot = items
        slots = page_table[:, tenant].astype(jnp.int32)
        a_in = adapter_in[ids, slots].astype(jnp.float32)
        b_down = adapter_down[ids, slots].astype(jnp.float32)
        rows_f = rows.astype(jnp.float32)
        pre = jnp.einsum('td,erd->ter', rows_f, a_in)
        gate = pre[:, :, :R]
        upv = pre[:, :, R:]
        sig = jax.nn.sigmoid(gate)
        act = gate * sig
        hidden = rounded(act * upv)
        select = (route[:, :, None] == ids[None, None, :]).astype(jnp.float32)
        masked = select[:, :, :, None] * hidden[:, None]
        branch = rounded(jnp.einsum('tker,erd->tkd', masked, b_down))
        adapted = jnp.sum(weight[:, :, None] * branch, axis=1).astype(jnp.bfloat16)
        cot_f = cot.astype(jnp.float32)
        weight_grad = jnp.sum(cot_f[:, None, :] * branch, axis=2)
        scaled = rounded(weight[:, :, None] * cot_f[:, None, :])
        hgrad = jnp.einsum('tkd,erd->tker', scaled, b_down) * select[:, :, :, None]
        gate_grad = hgrad * (upv * sig * (1.0 + gate * (1.0 - sig)))[:, None]
        up_grad = hgrad * act[:, None]
        lowrank = rounded(jnp.concatenate([gate_grad, up_grad], axis=3))
        input_grad = rounded(jnp.einsum('tker,erd->tkd', lowrank, a_in))
        token_grad = jnp.sum(input_grad, axis=1).astype(jnp.bfloat16)
        grad_in = grad_in.at[ids, slots].add(jnp.einsum('tker,td->erd', lowrank, rows_f))
        grad_down = grad_down.at[ids, slots].add(jnp.einsum('tker,tkd->erd', masked, scaled))
        return (grad_in, grad_down), (adapted, token_grad, weight_grad)

    items = (tokens.reshape(BLOCKS, TOK_DEV, D), routes.reshape(BLOCKS, TOK_DEV, TOP),
             route_weight.reshape(BLOCKS, TOK_DEV, TOP), block_tenant.astype(jnp.int32),
             upstream.reshape(BLOCKS, TOK_DEV, D))
    start = (jnp.zeros((EXPERTS, TENANTS, 2 * R, D), jnp.float32),
             jnp.zeros((EXPERTS, TENANTS, R, D), jnp.float32))
    (grad_in, grad_down), (adapted, grad_tokens, grad_weight) = lax.scan(step, start, items)
    return (adapted.reshape(TOKENS, D), grad_tokens.reshape(TOKENS, D),
            grad_weight.reshape(TOKENS, TOP), grad_in, grad_down)
```

```python
import functools

import jax
import jax.numpy as jnp
from jax import lax
from jax.experimental import pallas as pl
from jax.experimental.pallas import tpu as pltpu
from jax.sharding import PartitionSpec as P

BF16 = jnp.bfloat16
F32 = jnp.float32
MESH = pl.DeviceIdType.MESH
LAST_LAST = (((1,), (1,)), ((), ()))
PLAIN = (((1,), (0,)), ((), ()))


def matmul(left, right, dims=PLAIN):
    return lax.dot_general(left, right, dims, preferred_element_type=F32)


def step_order(size):
    return sorted(range(size), key=lambda step: -min(step, size - step))


def adapter_kernel(
    sizes,
    block_tenant, page_table, routes, weights, tokens, upstream, adapter_in, adapter_down,
    adapted, grad_tokens, grad_weight, grad_parts,
    all_in, all_down, tok, cot, pages_out, pages, sums_out, sums_in, proj_out, proj_in,
    parts_out, adapted_v, grad_tokens_v,
    load_sem, token_sem, page_send, page_recv, swap_send, swap_recv, part_send, part_recv,
    own_sem, out_sem,
):
    dp_size, ex_size, exp_dev, rank, piece, tok_dev, top = sizes
    wide = ex_size * exp_dev * rank
    me_dp = lax.axis_index("dp")
    me_ex = lax.axis_index("expert")
    other_core = lax.rem(lax.axis_index("tensor") + 1, 2)
    dp_order = step_order(dp_size)
    peers = [(dz, dx) for dz in dp_order for dx in range(ex_size) if (dz, dx) != (0, 0)]

    def dp_at(dz):
        return lax.rem(me_dp + dz, dp_size)

    def ex_at(dx):
        return lax.rem(me_ex + dx, ex_size)

    def columns(p):
        return pl.ds(p * piece, piece)

    load_in = pltpu.make_async_copy(adapter_in, all_in, load_sem.at[0])
    load_down = pltpu.make_async_copy(adapter_down, all_down, load_sem.at[1])
    load_in.start()
    load_down.start()
    token_loads = []
    for p in range(dp_size):
        token_loads.append(
            pltpu.make_async_copy(tokens.at[:, columns(p)], tok.at[p], token_sem.at[0, p])
        )
        token_loads.append(
            pltpu.make_async_copy(upstream.at[:, columns(p)], cot.at[p], token_sem.at[1, p])
        )
    for load in token_loads:
        load.start()

    barrier = pltpu.get_barrier_semaphore()
    for dz, dx in peers:
        pl.semaphore_signal(
            barrier, inc=1, device_id={"dp": dp_at(dz), "expert": ex_at(dx)}, device_id_type=MESH
        )
    pl.semaphore_signal(barrier, inc=1, device_id={"tensor": other_core}, device_id_type=MESH)
    pl.semaphore_wait(barrier, len(peers) + 1)

    def page_copy(dz, dx):
        return pltpu.make_async_remote_copy(
            src_ref=pages_out.at[dp_at(dz), ex_at(dx)],
            dst_ref=pages.at[me_dp, :, me_ex],
            send_sem=page_send.at[dz, dx],
            recv_sem=page_recv.at[me_dp, me_ex],
            device_id={"dp": dp_at(dz), "expert": ex_at(dx)},
            device_id_type=MESH,
        )

    def page_arrival(dz, dx):
        return pltpu.make_async_remote_copy(
            src_ref=pages_out.at[dp_at(dz), ex_at(dx)],
            dst_ref=pages.at[dp_at(dz), :, ex_at(dx)],
            send_sem=page_send.at[dz, dx],
            recv_sem=page_recv.at[dp_at(dz), ex_at(dx)],
            device_id={"dp": dp_at(dz), "expert": ex_at(dx)},
            device_id_type=MESH,
        )

    load_in.wait()
    load_down.wait()
    for dz, dx in peers + [(0, 0)]:
        tenant = block_tenant[dp_at(dz) * ex_size + ex_at(dx)]
        for local in range(exp_dev):
            slot = page_table[me_ex * exp_dev + local, tenant]
            page = all_in[local, slot]
            down = all_down[local, slot]
            rows = (page[:rank], page[rank:], down)
            for kind in range(3):
                if (dz, dx) == (0, 0):
                    pages[me_dp, kind, me_ex, local] = rows[kind]
                else:
                    pages_out[dp_at(dz), ex_at(dx), kind, local] = rows[kind]
        if (dz, dx) != (0, 0):
            page_copy(dz, dx).start()

    for load in token_loads:
        load.wait()
    pre = None
    for dz in [0] + dp_order[:-1]:
        for dx in range(ex_size):
            if (dz, dx) != (0, 0):
                page_arrival(dz, dx).wait_recv()
        d = dp_at(dz)
        pre_part = matmul(tok[d], pages[d, 0:2].reshape(2 * wide, piece), LAST_LAST)
        proj_part = matmul(cot[d], pages[d, 2].reshape(wide, piece), LAST_LAST)
        pre, proj = (pre_part, proj_part) if pre is None else (pre + pre_part, proj + proj_part)

    sums_out[...] = pre
    proj_out[...] = proj
    swaps = []
    for i, (out_ref, in_ref) in enumerate([(sums_out, sums_in), (proj_out, proj_in)]):
        swaps.append(
            pltpu.make_async_remote_copy(
                src_ref=out_ref,
                dst_ref=in_ref,
                send_sem=swap_send.at[i],
                recv_sem=swap_recv.at[i],
                device_id={"tensor": other_core},
                device_id_type=MESH,
            )
        )
        swaps[-1].start()
    expert_of = lax.broadcasted_iota(jnp.int32, (tok_dev, wide), 1) // rank
    chosen = [routes[:, k : k + 1] == expert_of for k in range(top)]
    weight = sum(jnp.where(chosen[k], weights[:, k : k + 1], 0.0) for k in range(top))
    for swap in swaps:
        swap.wait_recv()
    pre = pre + sums_in[...]
    proj = proj + proj_in[...]
    gate = pre[:, :wide]
    upv = pre[:, wide:]
    sig = jax.nn.sigmoid(gate)
    act = gate * sig
    hidden = (act * upv).astype(BF16).astype(F32)
    weighted = weight * hidden
    hgrad = weight * proj
    gate_grad = hgrad * upv * sig * (1.0 + gate * (1.0 - sig))
    up_grad = hgrad * act
    lowrank_t = jnp.concatenate([gate_grad.T, up_grad.T], axis=0).astype(BF16)
    weighted_t = weighted.T.astype(BF16)

    def part_copy(dz, dx, source):
        return pltpu.make_async_remote_copy(
            src_ref=parts_out.at[dp_at(dz), :, ex_at(dx)],
            dst_ref=grad_parts.at[source[0], source[1]],
            send_sem=part_send.at[dz, dx],
            recv_sem=part_recv.at[source[0], source[1]],
            device_id={"dp": dp_at(dz), "expert": ex_at(dx)},
            device_id_type=MESH,
        )

    own = pltpu.make_async_copy(
        parts_out.at[me_dp, :, me_ex], grad_parts.at[me_dp, me_ex], own_sem
    )
    for dz in dp_order:
        d = dp_at(dz)
        part = matmul(lowrank_t, tok[d]).astype(BF16)
        parts_out[d, 0:2] = part.reshape(2, ex_size, exp_dev, rank, piece)
        part = matmul(weighted_t, cot[d]).astype(BF16)
        parts_out[d, 2] = part.reshape(ex_size, exp_dev, rank, piece)
        for dx in range(ex_size):
            if (dz, dx) == (0, 0):
                own.start()
            else:
                part_copy(dz, dx, (me_dp, me_ex)).start()

    lowrank = jnp.concatenate([gate_grad, up_grad], axis=1).astype(BF16)
    weighted = weighted.astype(BF16)
    outs = []
    for p in range(dp_size):
        adapted_v[p] = matmul(weighted, pages[p, 2].reshape(wide, piece)).astype(BF16)
        outs.append(
            pltpu.make_async_copy(adapted_v.at[p], adapted.at[:, columns(p)], out_sem.at[0, p])
        )
        outs[-1].start()
        grad_tokens_v[p] = matmul(lowrank, pages[p, 0:2].reshape(2 * wide, piece)).astype(BF16)
        outs.append(
            pltpu.make_async_copy(
                grad_tokens_v.at[p], grad_tokens.at[:, columns(p)], out_sem.at[1, p]
            )
        )
        outs[-1].start()
    product = hidden * proj
    for k in range(top):
        grad_weight[:, k : k + 1] = jnp.sum(
            jnp.where(chosen[k], product, 0.0), axis=1, keepdims=True
        )

    for out in outs:
        out.wait()
    for swap in swaps:
        swap.wait_send()
    for dz, dx in peers:
        page_copy(dz, dx).wait_send()
    own.wait()
    for dz, dx in peers:
        part_copy(dz, dx, (me_dp, me_ex)).wait_send()
        part_copy(dz, dx, (dp_at(dz), ex_at(dx))).wait_recv()


def scatter_kernel(
    sizes, slots, block_tenant, page_table, parts, grad_in, grad_down
):
    dp_size, ex_size, exp_dev, rank = sizes
    local = pl.program_id(0)
    chunk = pl.program_id(1)
    grad_in[...] = jnp.zeros_like(grad_in)
    grad_down[...] = jnp.zeros_like(grad_down)
    expert = lax.axis_index("expert") * exp_dev + local
    for d in range(dp_size):
        for x in range(ex_size):
            place = page_table[expert, block_tenant[d * ex_size + x]] - chunk * slots

            @pl.when((place >= 0) & (place < slots))
            def _():
                grad_in[0, place, :rank] += parts[d, x, 0, local].astype(F32)
                grad_in[0, place, rank:] += parts[d, x, 1, local].astype(F32)
                grad_down[0, place] += parts[d, x, 2, local].astype(F32)


def paged(
    tokens, routes, route_weight, block_tenant, page_table, adapter_in, adapter_down, upstream
):
    tok_dev, half = tokens.shape
    top = routes.shape[1]
    exp_dev, tenants, _, piece = adapter_in.shape
    rank = adapter_down.shape[2]
    dp_size = lax.axis_size("dp")
    ex_size = lax.axis_size("expert")
    wide = ex_size * exp_dev * rank
    sizes = (dp_size, ex_size, exp_dev, rank, piece, tok_dev, top)
    any_spec = pl.BlockSpec(memory_space=pl.ANY)
    vmem_spec = pl.BlockSpec(memory_space=pltpu.VMEM)
    smem_spec = pl.BlockSpec(memory_space=pltpu.SMEM)
    dma = pltpu.SemaphoreType.DMA
    adapted, grad_tokens, grad_weight, parts = pl.pallas_call(
        functools.partial(adapter_kernel, sizes),
        out_shape=(
            jax.ShapeDtypeStruct((tok_dev, half), BF16),
            jax.ShapeDtypeStruct((tok_dev, half), BF16),
            jax.ShapeDtypeStruct((tok_dev, top), F32),
            jax.ShapeDtypeStruct((dp_size, ex_size, 3, exp_dev, rank, piece), BF16),
        ),
        in_specs=[smem_spec] * 2 + [vmem_spec] * 2 + [any_spec] * 4,
        out_specs=(any_spec, any_spec, vmem_spec, any_spec),
        scratch_shapes=[
            pltpu.VMEM(adapter_in.shape, BF16),
            pltpu.VMEM(adapter_down.shape, BF16),
            pltpu.VMEM((dp_size, tok_dev, piece), BF16),
            pltpu.VMEM((dp_size, tok_dev, piece), BF16),
            pltpu.VMEM((dp_size, ex_size, 3, exp_dev, rank, piece), BF16),
            pltpu.VMEM((dp_size, 3, ex_size, exp_dev, rank, piece), BF16),
            pltpu.VMEM((tok_dev, 2 * wide), F32),
            pltpu.VMEM((tok_dev, 2 * wide), F32),
            pltpu.VMEM((tok_dev, wide), F32),
            pltpu.VMEM((tok_dev, wide), F32),
            pltpu.VMEM((dp_size, 3, ex_size, exp_dev, rank, piece), BF16),
            pltpu.VMEM((dp_size, tok_dev, piece), BF16),
            pltpu.VMEM((dp_size, tok_dev, piece), BF16),
            dma((2,)),
            dma((2, dp_size)),
            dma((dp_size, ex_size)),
            dma((dp_size, ex_size)),
            dma((2,)),
            dma((2,)),
            dma((dp_size, ex_size)),
            dma((dp_size, ex_size)),
            dma,
            dma((2, dp_size)),
        ],
        compiler_params=pltpu.CompilerParams(
            collective_id=0, has_side_effects=True, vmem_limit_bytes=40 << 20
        ),
    )(
        block_tenant, page_table, routes, route_weight,
        tokens, upstream, adapter_in, adapter_down,
    )
    slots = 8
    grad_in, grad_down = pl.pallas_call(
        functools.partial(scatter_kernel, (dp_size, ex_size, exp_dev, rank), slots),
        grid=(exp_dev, tenants // slots),
        out_shape=(
            jax.ShapeDtypeStruct((exp_dev, tenants, 2 * rank, piece), F32),
            jax.ShapeDtypeStruct((exp_dev, tenants, rank, piece), F32),
        ),
        in_specs=[
            smem_spec,
            smem_spec,
            vmem_spec,
        ],
        out_specs=(
            pl.BlockSpec((1, slots, 2 * rank, piece), lambda i, j: (i, j, 0, 0)),
            pl.BlockSpec((1, slots, rank, piece), lambda i, j: (i, j, 0, 0)),
        ),
        compiler_params=pltpu.CompilerParams(vmem_limit_bytes=24 << 20),
    )(block_tenant, page_table, parts)
    return (adapted, grad_tokens, grad_weight, grad_in, grad_down)


def feature_sum(partial_value):
    return lax.psum(partial_value, "tensor")


def swap_blocks(block):
    return lax.all_to_all(block, "expert", split_axis=0, concat_axis=0, tiled=True)


def routed(
    tokens, routes, route_weight, block_tenant, page_table, adapter_in, adapter_down, upstream
):
    tok_dev, half = tokens.shape
    top = routes.shape[1]
    exp_dev = adapter_in.shape[0]
    tenants = adapter_in.shape[1]
    rank = adapter_down.shape[2]
    piece = adapter_in.shape[3]
    dp_size = lax.axis_size("dp")
    ex_size = lax.axis_size("expert")
    experts = exp_dev * ex_size
    column = lax.axis_index("expert")
    tenant_grid = block_tenant.reshape(dp_size, ex_size)
    local_table = lax.dynamic_slice_in_dim(page_table, column * exp_dev, exp_dev, 0)
    wanted = local_table[:, tenant_grid]
    flat_in = adapter_in.reshape(exp_dev, tenants, 2 * rank * piece)
    flat_down = adapter_down.reshape(exp_dev, tenants, rank * piece)
    send_in = jnp.stack([flat_in[local][wanted[local]] for local in range(exp_dev)], axis=1)
    send_down = jnp.stack([flat_down[local][wanted[local]] for local in range(exp_dev)], axis=1)
    got_in, got_down = (
        lax.all_to_all(send_in, "dp", split_axis=0, concat_axis=0, tiled=True),
        lax.all_to_all(send_down, "dp", split_axis=0, concat_axis=0, tiled=True),
    )
    page_in = (
        got_in.reshape(dp_size, exp_dev, ex_size, 2 * rank, piece)
        .transpose(1, 2, 3, 0, 4)
        .reshape(exp_dev, ex_size, 2 * rank, half)
    )
    page_down = (
        got_down.reshape(dp_size, exp_dev, ex_size, rank, piece)
        .transpose(1, 2, 3, 0, 4)
        .reshape(exp_dev, ex_size, rank, half)
    )
    scaled = (route_weight[:, :, None] * upstream[:, None, :].astype(jnp.float32)).astype(
        jnp.bfloat16
    )
    cap = 5 * tok_dev * top // (4 * experts)
    slot_count = experts * cap
    flat_routes = routes.reshape(-1)
    hits = (flat_routes[:, None] == jnp.arange(experts, dtype=jnp.int32)[None, :]).astype(jnp.int32)
    position = jnp.sum((jnp.cumsum(hits, axis=0) - 1) * hits, axis=1)
    slot = flat_routes * cap + position
    placing = (slot[None, :] == jnp.arange(slot_count, dtype=jnp.int32)[:, None]).astype(
        jnp.bfloat16
    )
    placing_tok = jnp.sum(placing.reshape(slot_count, tok_dev, top), axis=2)
    rows_send = jnp.dot(placing_tok, tokens, preferred_element_type=jnp.float32).astype(
        jnp.bfloat16
    )
    arrived = swap_blocks(rows_send).reshape(ex_size, exp_dev, cap, half)
    pre = feature_sum(
        jnp.einsum("kecd,ekrd->kecr", arrived, page_in, preferred_element_type=jnp.float32)
    )
    gate = pre[..., :rank]
    upv = pre[..., rank:]
    sig = jax.nn.sigmoid(gate)
    act = gate * sig
    hidden = (act * upv).astype(jnp.bfloat16)
    branch = jnp.einsum(
        "kecr,ekrd->kecd", hidden, page_down, preferred_element_type=jnp.float32
    ).astype(jnp.bfloat16)
    returned = swap_blocks(branch.reshape(slot_count, half))
    picked = returned[slot].reshape(tok_dev, top, half)
    adapted = jnp.sum(route_weight[:, :, None] * picked.astype(jnp.float32), axis=1).astype(
        jnp.bfloat16
    )
    grad_weight = feature_sum(
        jnp.einsum("td,tkd->tk", upstream, picked, preferred_element_type=jnp.float32)
    )
    cot_send = jnp.dot(
        placing, scaled.reshape(tok_dev * top, half), preferred_element_type=jnp.float32
    ).astype(jnp.bfloat16)
    cot_blocks = swap_blocks(cot_send).reshape(ex_size, exp_dev, cap, half)
    hgrad = feature_sum(
        jnp.einsum("kecd,ekrd->kecr", cot_blocks, page_down, preferred_element_type=jnp.float32)
    )
    lowrank = jnp.concatenate(
        [hgrad * upv * sig * (1.0 + gate * (1.0 - sig)), hgrad * act], axis=3
    ).astype(jnp.bfloat16)
    input_grad = jnp.einsum(
        "kecr,ekrd->kecd", lowrank, page_in, preferred_element_type=jnp.float32
    ).astype(jnp.bfloat16)
    req_in = jnp.einsum("kecr,kecd->ekrd", lowrank, arrived, preferred_element_type=jnp.float32)
    req_down = jnp.einsum("kecr,kecd->ekrd", hidden, cot_blocks, preferred_element_type=jnp.float32)
    grad_back = swap_blocks(input_grad.reshape(slot_count, half))
    grad_tokens = jnp.sum(
        grad_back[slot].reshape(tok_dev, top, half).astype(jnp.float32), axis=1
    ).astype(jnp.bfloat16)
    out_in = (
        req_in.reshape(exp_dev, ex_size, 2 * rank, dp_size, piece)
        .transpose(3, 0, 1, 2, 4)
        .reshape(dp_size, exp_dev, ex_size, 2 * rank * piece)
    )
    out_down = (
        req_down.reshape(exp_dev, ex_size, rank, dp_size, piece)
        .transpose(3, 0, 1, 2, 4)
        .reshape(dp_size, exp_dev, ex_size, rank * piece)
    )
    recv_in, recv_down = (
        lax.all_to_all(out_in, "dp", split_axis=0, concat_axis=0, tiled=True),
        lax.all_to_all(out_down, "dp", split_axis=0, concat_axis=0, tiled=True),
    )
    sums_in = []
    sums_down = []
    for local in range(exp_dev):
        owners = wanted[local].reshape(-1)
        sums_in.append(
            jnp.zeros((tenants, 2 * rank * piece), jnp.float32)
            .at[owners]
            .add(recv_in[:, local].reshape(dp_size * ex_size, -1))
        )
        sums_down.append(
            jnp.zeros((tenants, rank * piece), jnp.float32)
            .at[owners]
            .add(recv_down[:, local].reshape(dp_size * ex_size, -1))
        )
    grad_in = jnp.stack(sums_in, axis=0).reshape(exp_dev, tenants, 2 * rank, piece)
    grad_down = jnp.stack(sums_down, axis=0).reshape(exp_dev, tenants, rank, piece)
    return (adapted, grad_tokens, grad_weight, grad_in, grad_down)


def shards(*arrays):
    rank, piece = arrays[6].shape[2:]
    whole_tiles = piece % 128 == 0 and rank % 16 == 0 and lax.axis_size("tensor") == 2
    return paged(*arrays) if whole_tiles else routed(*arrays)


def solution(mesh):
    return jax.shard_map(
        shards,
        mesh=mesh,
        in_specs=(
            P(("groups", "dp", "expert"), "tensor"),
            P(("groups", "dp", "expert"), None),
            P(("groups", "dp", "expert"), None),
            P("groups"),
            P(),
            P("expert", None, None, ("tensor", "dp")),
            P("expert", None, None, ("tensor", "dp")),
            P(("groups", "dp", "expert"), "tensor"),
        ),
        out_specs=(
            P(("groups", "dp", "expert"), "tensor"),
            P(("groups", "dp", "expert"), "tensor"),
            P(("groups", "dp", "expert"), None),
            P(("groups", "expert"), None, None, ("tensor", "dp")),
            P(("groups", "expert"), None, None, ("tensor", "dp")),
        ),
        check_vma=False,
    )
```

```python
import functools

import jax
import jax.numpy as jnp
from jax import lax
from jax.experimental import pallas as pl
from jax.experimental.pallas import tpu as pltpu
from jax.sharding import PartitionSpec as P

BF16 = jnp.bfloat16
F32 = jnp.float32
MESH = pl.DeviceIdType.MESH
LAST_LAST = (((1,), (1,)), ((), ()))
PLAIN = (((1,), (0,)), ((), ()))


def matmul(left, right, dims=PLAIN):
    return lax.dot_general(left, right, dims, preferred_element_type=F32)


def step_order(size):
    return sorted(range(size), key=lambda step: -min(step, size - step))


def adapter_kernel(
    sizes,
    block_tenant, page_table, routes, weights, tokens, upstream, adapter_in, adapter_down,
    adapted, grad_tokens, grad_weight, grad_parts,
    tenants, table, route, weight_of,
    all_in, all_down, tok, cot, pages_out, pages, sums_out, sums_in, proj_out, proj_in,
    parts_out, adapted_v, grad_tokens_v, grad_weight_v,
    small_sem, load_sem, token_sem, page_send, page_recv, swap_send, swap_recv,
    part_send, part_recv, own_sem, out_sem,
):
    dp_size, ex_size, exp_dev, rank, piece, tok_dev, top = sizes
    wide = ex_size * exp_dev * rank
    kinds = (pl.ds(0, 2), pl.ds(2, 1))
    me_dp = lax.axis_index("dp")
    me_ex = lax.axis_index("expert")
    other_core = lax.rem(lax.axis_index("tensor") + 1, 2)
    dp_order = step_order(dp_size)
    peers = [(dz, dx) for dz in dp_order for dx in range(ex_size) if (dz, dx) != (0, 0)]

    def dp_at(dz):
        return lax.rem(me_dp + dz, dp_size)

    def ex_at(dx):
        return lax.rem(me_ex + dx, ex_size)

    def columns(p):
        return pl.ds(p * piece, piece)

    barrier = pltpu.get_barrier_semaphore()
    for dz, dx in peers:
        pl.semaphore_signal(
            barrier, inc=1, device_id={"dp": dp_at(dz), "expert": ex_at(dx)}, device_id_type=MESH
        )
    pl.semaphore_signal(barrier, inc=1, device_id={"tensor": other_core}, device_id_type=MESH)

    small_loads = [
        pltpu.make_async_copy(source, target, small_sem.at[i])
        for i, (source, target) in enumerate(
            [(block_tenant, tenants), (page_table, table), (routes, route), (weights, weight_of)]
        )
    ]
    load_in = pltpu.make_async_copy(adapter_in, all_in, load_sem.at[0])
    load_down = pltpu.make_async_copy(adapter_down, all_down, load_sem.at[1])
    tok_loads = [
        pltpu.make_async_copy(tokens.at[:, columns(p)], tok.at[p], token_sem.at[0, p])
        for p in range(dp_size)
    ]
    cot_loads = [
        pltpu.make_async_copy(upstream.at[:, columns(p)], cot.at[p], token_sem.at[1, p])
        for p in range(dp_size)
    ]
    for load in small_loads + [load_in, load_down] + tok_loads + cot_loads:
        load.start()

    def page_copy(i, dz, dx, place):
        return pltpu.make_async_remote_copy(
            src_ref=pages_out.at[dp_at(dz), ex_at(dx), kinds[i]],
            dst_ref=pages.at[place[0], kinds[i], place[1]],
            send_sem=page_send.at[i, dz, dx],
            recv_sem=page_recv.at[i, place[0], place[1]],
            device_id={"dp": dp_at(dz), "expert": ex_at(dx)},
            device_id_type=MESH,
        )

    def part_copy(i, dz, dx, place):
        return pltpu.make_async_remote_copy(
            src_ref=parts_out.at[dp_at(dz), kinds[i], ex_at(dx)],
            dst_ref=grad_parts.at[place[0], place[1], kinds[i]],
            send_sem=part_send.at[i, dz, dx],
            recv_sem=part_recv.at[i, place[0], place[1]],
            device_id={"dp": dp_at(dz), "expert": ex_at(dx)},
            device_id_type=MESH,
        )

    def swap_copy(i, out_ref, in_ref):
        return pltpu.make_async_remote_copy(
            src_ref=out_ref,
            dst_ref=in_ref,
            send_sem=swap_send.at[i],
            recv_sem=swap_recv.at[i],
            device_id={"tensor": other_core},
            device_id_type=MESH,
        )

    def send_pages(i):
        for dz, dx in peers + [(0, 0)]:
            tenant = tenants[dp_at(dz) * ex_size + ex_at(dx)]
            for local in range(exp_dev):
                slot = table[me_ex * exp_dev + local, tenant]
                if i == 0:
                    page = all_in[local, slot]
                    rows = {0: page[:rank], 1: page[rank:]}
                else:
                    rows = {2: all_down[local, slot]}
                for kind, value in rows.items():
                    if (dz, dx) == (0, 0):
                        pages[me_dp, kind, me_ex, local] = value
                    else:
                        pages_out[dp_at(dz), ex_at(dx), kind, local] = value
            if (dz, dx) != (0, 0):
                page_copy(i, dz, dx, (me_dp, me_ex)).start()

    def project(i, rows):
        total = None
        for dz in [0] + dp_order[:-1]:
            d = dp_at(dz)
            for dx in range(ex_size):
                if (dz, dx) != (0, 0):
                    page_copy(i, dz, dx, (d, ex_at(dx))).wait_recv()
            page = pages[d, 0:2] if i == 0 else pages[d, 2]
            part = matmul(page.reshape(-1, piece), rows[d], LAST_LAST)
            total = part if total is None else total + part
        return total

    def send_parts(i, values, rows):
        for dz in dp_order:
            d = dp_at(dz)
            part = matmul(values, rows[d]).astype(BF16)
            if i == 0:
                parts_out[d, 0:2] = part.reshape(2, ex_size, exp_dev, rank, piece)
            else:
                parts_out[d, 2] = part.reshape(ex_size, exp_dev, rank, piece)
            for dx in range(ex_size):
                if (dz, dx) != (0, 0):
                    part_copy(i, dz, dx, (me_dp, me_ex)).start()

    small_loads[0].wait()
    small_loads[1].wait()
    load_in.wait()
    pl.semaphore_wait(barrier, len(peers) + 1)
    send_pages(0)
    load_down.wait()
    send_pages(1)

    for load in small_loads[2:] + tok_loads:
        load.wait()
    expert_of = lax.broadcasted_iota(jnp.int32, (wide, tok_dev), 0) // rank
    chosen = [route[k : k + 1, :] == expert_of for k in range(top)]
    weight = sum(jnp.where(chosen[k], weight_of[k : k + 1, :], 0.0) for k in range(top))
    pre = project(0, tok)
    sums_out[...] = pre
    swap_pre = swap_copy(0, sums_out, sums_in)
    swap_pre.start()
    for load in cot_loads:
        load.wait()
    swap_pre.wait_recv()
    pre = pre + sums_in[...]
    gate = pre[:wide]
    upv = pre[wide:]
    sig = jax.nn.sigmoid(gate)
    act = gate * sig
    hidden = (act * upv).astype(BF16).astype(F32)
    weighted = weight * hidden
    send_parts(1, weighted.astype(BF16), cot)

    proj = project(1, cot)
    proj_out[...] = proj
    swap_proj = swap_copy(1, proj_out, proj_in)
    swap_proj.start()
    swap_proj.wait_recv()
    proj = proj + proj_in[...]
    hgrad = weight * proj
    lowrank = jnp.concatenate(
        [hgrad * upv * sig * (1.0 + gate * (1.0 - sig)), hgrad * act], axis=0
    )
    send_parts(0, lowrank.astype(BF16), tok)
    own = pltpu.make_async_copy(
        parts_out.at[me_dp, :, me_ex], grad_parts.at[me_dp, me_ex], own_sem
    )
    own.start()

    weighted = weighted.T.astype(BF16)
    lowrank = lowrank.T.astype(BF16)
    outs = []
    for p in range(dp_size):
        adapted_v[p] = matmul(weighted, pages[p, 2].reshape(wide, piece)).astype(BF16)
        outs.append(
            pltpu.make_async_copy(adapted_v.at[p], adapted.at[:, columns(p)], out_sem.at[0, p])
        )
        outs[-1].start()
        grad_tokens_v[p] = matmul(lowrank, pages[p, 0:2].reshape(2 * wide, piece)).astype(BF16)
        outs.append(
            pltpu.make_async_copy(
                grad_tokens_v.at[p], grad_tokens.at[:, columns(p)], out_sem.at[1, p]
            )
        )
        outs[-1].start()
    product = hidden * proj
    for k in range(top):
        grad_weight_v[k : k + 1, :] = jnp.sum(
            jnp.where(chosen[k], product, 0.0), axis=0, keepdims=True
        )
    outs.append(pltpu.make_async_copy(grad_weight_v, grad_weight, out_sem.at[2, 0]))
    outs[-1].start()

    for out in outs:
        out.wait()
    swap_pre.wait_send()
    swap_proj.wait_send()
    own.wait()
    for i in range(2):
        for dz, dx in peers:
            page_copy(i, dz, dx, (me_dp, me_ex)).wait_send()
    for i in (1, 0):
        for dz, dx in peers:
            part_copy(i, dz, dx, (me_dp, me_ex)).wait_send()
            part_copy(i, dz, dx, (dp_at(dz), ex_at(dx))).wait_recv()


def scatter_kernel(
    sizes, slots,
    block_tenant, page_table, parts, adapted, grad_tokens,
    grad_in, grad_down, adapted_out, grad_tokens_out,
    tenants, table, parts_v, small_sem, parts_sem, pass_sem,
):
    dp_size, ex_size, exp_dev, rank = sizes
    local = pl.program_id(0)
    chunk = pl.program_id(1)
    loads = [
        pltpu.make_async_copy(block_tenant, tenants, small_sem.at[0]),
        pltpu.make_async_copy(page_table, table, small_sem.at[1]),
        pltpu.make_async_copy(parts, parts_v, parts_sem),
    ]
    passed = [
        pltpu.make_async_copy(adapted, adapted_out, pass_sem.at[0]),
        pltpu.make_async_copy(grad_tokens, grad_tokens_out, pass_sem.at[1]),
    ]
    first = (local == 0) & (chunk == 0)

    @pl.when(first)
    def _():
        for load in loads + passed:
            load.start()

    grad_in[...] = jnp.zeros_like(grad_in)
    grad_down[...] = jnp.zeros_like(grad_down)

    @pl.when(first)
    def _():
        for load in loads:
            load.wait()

    expert = lax.axis_index("expert") * exp_dev + local
    for d in range(dp_size):
        for x in range(ex_size):
            place = table[expert, tenants[d * ex_size + x]] - chunk * slots

            @pl.when((place >= 0) & (place < slots))
            def _():
                grad_in[0, place, :rank] += parts_v[d, x, 0, local].astype(F32)
                grad_in[0, place, rank:] += parts_v[d, x, 1, local].astype(F32)
                grad_down[0, place] += parts_v[d, x, 2, local].astype(F32)

    @pl.when((local == pl.num_programs(0) - 1) & (chunk == pl.num_programs(1) - 1))
    def _():
        for copy in passed:
            copy.wait()


def paged(
    tokens, routes, route_weight, block_tenant, page_table, adapter_in, adapter_down, upstream
):
    tok_dev, half = tokens.shape
    top = routes.shape[1]
    exp_dev, tenants, _, piece = adapter_in.shape
    rank = adapter_down.shape[2]
    dp_size = lax.axis_size("dp")
    ex_size = lax.axis_size("expert")
    wide = ex_size * exp_dev * rank
    sizes = (dp_size, ex_size, exp_dev, rank, piece, tok_dev, top)
    any_spec = pl.BlockSpec(memory_space=pl.ANY)
    dma = pltpu.SemaphoreType.DMA
    parts_shape = (dp_size, ex_size, 3, exp_dev, rank, piece)
    rows_shape = jax.ShapeDtypeStruct((tok_dev, half), BF16)
    small_scratch = [
        pltpu.SMEM(block_tenant.shape, jnp.int32),
        pltpu.SMEM(page_table.shape, jnp.int32),
    ]
    adapted, grad_tokens, grad_weight, parts = pl.pallas_call(
        functools.partial(adapter_kernel, sizes),
        out_shape=(
            rows_shape,
            rows_shape,
            jax.ShapeDtypeStruct((top, tok_dev), F32),
            jax.ShapeDtypeStruct(parts_shape, BF16),
        ),
        in_specs=[any_spec] * 8,
        out_specs=(any_spec,) * 4,
        scratch_shapes=small_scratch
        + [
            pltpu.VMEM((top, tok_dev), jnp.int32),
            pltpu.VMEM((top, tok_dev), F32),
            pltpu.VMEM(adapter_in.shape, BF16),
            pltpu.VMEM(adapter_down.shape, BF16),
            pltpu.VMEM((dp_size, tok_dev, piece), BF16),
            pltpu.VMEM((dp_size, tok_dev, piece), BF16),
            pltpu.VMEM(parts_shape, BF16),
            pltpu.VMEM((dp_size, 3, ex_size, exp_dev, rank, piece), BF16),
            pltpu.VMEM((2 * wide, tok_dev), F32),
            pltpu.VMEM((2 * wide, tok_dev), F32),
            pltpu.VMEM((wide, tok_dev), F32),
            pltpu.VMEM((wide, tok_dev), F32),
            pltpu.VMEM((dp_size, 3, ex_size, exp_dev, rank, piece), BF16),
            pltpu.VMEM((dp_size, tok_dev, piece), BF16),
            pltpu.VMEM((dp_size, tok_dev, piece), BF16),
            pltpu.VMEM((top, tok_dev), F32),
            dma((4,)),
            dma((2,)),
            dma((2, dp_size)),
            dma((2, dp_size, ex_size)),
            dma((2, dp_size, ex_size)),
            dma((2,)),
            dma((2,)),
            dma((2, dp_size, ex_size)),
            dma((2, dp_size, ex_size)),
            dma,
            dma((3, dp_size)),
        ],
        compiler_params=pltpu.CompilerParams(
            collective_id=0, has_side_effects=True, vmem_limit_bytes=60 << 20
        ),
    )(
        block_tenant, page_table, routes.T, route_weight.T,
        tokens, upstream, adapter_in, adapter_down,
    )
    slots = 8
    grad_in, grad_down, adapted, grad_tokens = pl.pallas_call(
        functools.partial(scatter_kernel, (dp_size, ex_size, exp_dev, rank), slots),
        grid=(exp_dev, tenants // slots),
        out_shape=(
            jax.ShapeDtypeStruct((exp_dev, tenants, 2 * rank, piece), F32),
            jax.ShapeDtypeStruct((exp_dev, tenants, rank, piece), F32),
            rows_shape,
            rows_shape,
        ),
        in_specs=[any_spec] * 5,
        out_specs=(
            pl.BlockSpec((1, slots, 2 * rank, piece), lambda i, j: (i, j, 0, 0)),
            pl.BlockSpec((1, slots, rank, piece), lambda i, j: (i, j, 0, 0)),
            any_spec,
            any_spec,
        ),
        scratch_shapes=small_scratch
        + [pltpu.VMEM(parts_shape, BF16), dma((2,)), dma, dma((2,))],
        compiler_params=pltpu.CompilerParams(vmem_limit_bytes=60 << 20),
    )(block_tenant, page_table, parts, adapted, grad_tokens)
    return (adapted, grad_tokens, grad_weight.T, grad_in, grad_down)


def feature_sum(partial_value):
    return lax.psum(partial_value, "tensor")


def swap_blocks(block):
    return lax.all_to_all(block, "expert", split_axis=0, concat_axis=0, tiled=True)


def routed(
    tokens, routes, route_weight, block_tenant, page_table, adapter_in, adapter_down, upstream
):
    tok_dev, half = tokens.shape
    top = routes.shape[1]
    exp_dev = adapter_in.shape[0]
    tenants = adapter_in.shape[1]
    rank = adapter_down.shape[2]
    piece = adapter_in.shape[3]
    dp_size = lax.axis_size("dp")
    ex_size = lax.axis_size("expert")
    experts = exp_dev * ex_size
    column = lax.axis_index("expert")
    tenant_grid = block_tenant.reshape(dp_size, ex_size)
    local_table = lax.dynamic_slice_in_dim(page_table, column * exp_dev, exp_dev, 0)
    wanted = local_table[:, tenant_grid]
    flat_in = adapter_in.reshape(exp_dev, tenants, 2 * rank * piece)
    flat_down = adapter_down.reshape(exp_dev, tenants, rank * piece)
    send_in = jnp.stack([flat_in[local][wanted[local]] for local in range(exp_dev)], axis=1)
    send_down = jnp.stack([flat_down[local][wanted[local]] for local in range(exp_dev)], axis=1)
    got_in, got_down = (
        lax.all_to_all(send_in, "dp", split_axis=0, concat_axis=0, tiled=True),
        lax.all_to_all(send_down, "dp", split_axis=0, concat_axis=0, tiled=True),
    )
    page_in = (
        got_in.reshape(dp_size, exp_dev, ex_size, 2 * rank, piece)
        .transpose(1, 2, 3, 0, 4)
        .reshape(exp_dev, ex_size, 2 * rank, half)
    )
    page_down = (
        got_down.reshape(dp_size, exp_dev, ex_size, rank, piece)
        .transpose(1, 2, 3, 0, 4)
        .reshape(exp_dev, ex_size, rank, half)
    )
    scaled = (route_weight[:, :, None] * upstream[:, None, :].astype(jnp.float32)).astype(
        jnp.bfloat16
    )
    cap = 5 * tok_dev * top // (4 * experts)
    slot_count = experts * cap
    flat_routes = routes.reshape(-1)
    hits = (flat_routes[:, None] == jnp.arange(experts, dtype=jnp.int32)[None, :]).astype(jnp.int32)
    position = jnp.sum((jnp.cumsum(hits, axis=0) - 1) * hits, axis=1)
    slot = flat_routes * cap + position
    placing = (slot[None, :] == jnp.arange(slot_count, dtype=jnp.int32)[:, None]).astype(
        jnp.bfloat16
    )
    placing_tok = jnp.sum(placing.reshape(slot_count, tok_dev, top), axis=2)
    rows_send = jnp.dot(placing_tok, tokens, preferred_element_type=jnp.float32).astype(
        jnp.bfloat16
    )
    arrived = swap_blocks(rows_send).reshape(ex_size, exp_dev, cap, half)
    pre = feature_sum(
        jnp.einsum("kecd,ekrd->kecr", arrived, page_in, preferred_element_type=jnp.float32)
    )
    gate = pre[..., :rank]
    upv = pre[..., rank:]
    sig = jax.nn.sigmoid(gate)
    act = gate * sig
    hidden = (act * upv).astype(jnp.bfloat16)
    branch = jnp.einsum(
        "kecr,ekrd->kecd", hidden, page_down, preferred_element_type=jnp.float32
    ).astype(jnp.bfloat16)
    returned = swap_blocks(branch.reshape(slot_count, half))
    picked = returned[slot].reshape(tok_dev, top, half)
    adapted = jnp.sum(route_weight[:, :, None] * picked.astype(jnp.float32), axis=1).astype(
        jnp.bfloat16
    )
    grad_weight = feature_sum(
        jnp.einsum("td,tkd->tk", upstream, picked, preferred_element_type=jnp.float32)
    )
    cot_send = jnp.dot(
        placing, scaled.reshape(tok_dev * top, half), preferred_element_type=jnp.float32
    ).astype(jnp.bfloat16)
    cot_blocks = swap_blocks(cot_send).reshape(ex_size, exp_dev, cap, half)
    hgrad = feature_sum(
        jnp.einsum("kecd,ekrd->kecr", cot_blocks, page_down, preferred_element_type=jnp.float32)
    )
    lowrank = jnp.concatenate(
        [hgrad * upv * sig * (1.0 + gate * (1.0 - sig)), hgrad * act], axis=3
    ).astype(jnp.bfloat16)
    input_grad = jnp.einsum(
        "kecr,ekrd->kecd", lowrank, page_in, preferred_element_type=jnp.float32
    ).astype(jnp.bfloat16)
    req_in = jnp.einsum("kecr,kecd->ekrd", lowrank, arrived, preferred_element_type=jnp.float32)
    req_down = jnp.einsum("kecr,kecd->ekrd", hidden, cot_blocks, preferred_element_type=jnp.float32)
    grad_back = swap_blocks(input_grad.reshape(slot_count, half))
    grad_tokens = jnp.sum(
        grad_back[slot].reshape(tok_dev, top, half).astype(jnp.float32), axis=1
    ).astype(jnp.bfloat16)
    out_in = (
        req_in.reshape(exp_dev, ex_size, 2 * rank, dp_size, piece)
        .transpose(3, 0, 1, 2, 4)
        .reshape(dp_size, exp_dev, ex_size, 2 * rank * piece)
    )
    out_down = (
        req_down.reshape(exp_dev, ex_size, rank, dp_size, piece)
        .transpose(3, 0, 1, 2, 4)
        .reshape(dp_size, exp_dev, ex_size, rank * piece)
    )
    recv_in, recv_down = (
        lax.all_to_all(out_in, "dp", split_axis=0, concat_axis=0, tiled=True),
        lax.all_to_all(out_down, "dp", split_axis=0, concat_axis=0, tiled=True),
    )
    sums_in = []
    sums_down = []
    for local in range(exp_dev):
        owners = wanted[local].reshape(-1)
        sums_in.append(
            jnp.zeros((tenants, 2 * rank * piece), jnp.float32)
            .at[owners]
            .add(recv_in[:, local].reshape(dp_size * ex_size, -1))
        )
        sums_down.append(
            jnp.zeros((tenants, rank * piece), jnp.float32)
            .at[owners]
            .add(recv_down[:, local].reshape(dp_size * ex_size, -1))
        )
    grad_in = jnp.stack(sums_in, axis=0).reshape(exp_dev, tenants, 2 * rank, piece)
    grad_down = jnp.stack(sums_down, axis=0).reshape(exp_dev, tenants, rank, piece)
    return (adapted, grad_tokens, grad_weight, grad_in, grad_down)


def shards(*arrays):
    rank, piece = arrays[6].shape[2:]
    whole_tiles = piece % 128 == 0 and rank % 16 == 0 and lax.axis_size("tensor") == 2
    return paged(*arrays) if whole_tiles else routed(*arrays)


def solution(mesh):
    return jax.shard_map(
        shards,
        mesh=mesh,
        in_specs=(
            P(("groups", "dp", "expert"), "tensor"),
            P(("groups", "dp", "expert"), None),
            P(("groups", "dp", "expert"), None),
            P("groups"),
            P(),
            P("expert", None, None, ("tensor", "dp")),
            P("expert", None, None, ("tensor", "dp")),
            P(("groups", "dp", "expert"), "tensor"),
        ),
        out_specs=(
            P(("groups", "dp", "expert"), "tensor"),
            P(("groups", "dp", "expert"), "tensor"),
            P(("groups", "dp", "expert"), None),
            P(("groups", "expert"), None, None, ("tensor", "dp")),
            P(("groups", "expert"), None, None, ("tensor", "dp")),
        ),
        check_vma=False,
    )
```

```python
import functools

import jax
import jax.numpy as jnp
from jax import lax
from jax.experimental import pallas as pl
from jax.experimental.pallas import tpu as pltpu
from jax.sharding import PartitionSpec as P

BF16 = jnp.bfloat16
F32 = jnp.float32
MESH = pl.DeviceIdType.MESH
LAST_LAST = (((1,), (1,)), ((), ()))
PLAIN = (((1,), (0,)), ((), ()))


def matmul(left, right, dims=PLAIN):
    return lax.dot_general(left, right, dims, preferred_element_type=F32)


def step_order(size):
    return sorted(range(size), key=lambda step: -min(step, size - step))


def adapter_kernel(
    sizes,
    block_tenant, page_table, routes, weights, tokens, upstream, adapter_in, adapter_down,
    adapted, grad_tokens, grad_weight, grad_parts,
    tenants, table, route, weight_of,
    all_in, all_down, tok, cot, pages_out, pages, sums_out, sums_in, proj_out, proj_in,
    parts_out, adapted_v, grad_tokens_v, grad_weight_v,
    small_sem, load_sem, token_sem, page_send, page_recv, swap_send, swap_recv,
    part_send, part_recv, own_sem, out_sem,
):
    dp_size, ex_size, exp_dev, rank, piece, tok_dev, top = sizes
    wide = ex_size * exp_dev * rank
    kinds = (pl.ds(0, 2), pl.ds(2, 1))
    me_dp = lax.axis_index("dp")
    me_ex = lax.axis_index("expert")
    other_core = lax.rem(lax.axis_index("tensor") + 1, 2)
    dp_order = step_order(dp_size)
    peers = [(dz, dx) for dz in dp_order for dx in range(ex_size) if (dz, dx) != (0, 0)]

    def dp_at(dz):
        return lax.rem(me_dp + dz, dp_size)

    def ex_at(dx):
        return lax.rem(me_ex + dx, ex_size)

    def columns(p):
        return pl.ds(p * piece, piece)

    barrier = pltpu.get_barrier_semaphore()
    for dz, dx in peers:
        pl.semaphore_signal(
            barrier, inc=1, device_id={"dp": dp_at(dz), "expert": ex_at(dx)}, device_id_type=MESH
        )
    pl.semaphore_signal(barrier, inc=1, device_id={"tensor": other_core}, device_id_type=MESH)

    small_loads = [
        pltpu.make_async_copy(source, target, small_sem.at[i])
        for i, (source, target) in enumerate(
            [(block_tenant, tenants), (page_table, table), (routes, route), (weights, weight_of)]
        )
    ]
    load_in = pltpu.make_async_copy(adapter_in, all_in, load_sem.at[0])
    load_down = pltpu.make_async_copy(adapter_down, all_down, load_sem.at[1])
    tok_loads = [
        pltpu.make_async_copy(tokens.at[:, columns(p)], tok.at[p], token_sem.at[0, p])
        for p in range(dp_size)
    ]
    cot_loads = [
        pltpu.make_async_copy(upstream.at[:, columns(p)], cot.at[p], token_sem.at[1, p])
        for p in range(dp_size)
    ]
    for load in small_loads + [load_in, load_down] + tok_loads + cot_loads:
        load.start()

    def page_copy(i, dz, dx, place):
        return pltpu.make_async_remote_copy(
            src_ref=pages_out.at[dp_at(dz), ex_at(dx), kinds[i]],
            dst_ref=pages.at[place[0], kinds[i], place[1]],
            send_sem=page_send.at[i, dz, dx],
            recv_sem=page_recv.at[i, place[0], place[1]],
            device_id={"dp": dp_at(dz), "expert": ex_at(dx)},
            device_id_type=MESH,
        )

    def part_copy(i, dz, dx, place):
        return pltpu.make_async_remote_copy(
            src_ref=parts_out.at[dp_at(dz), kinds[i], ex_at(dx)],
            dst_ref=grad_parts.at[place[0], place[1], kinds[i]],
            send_sem=part_send.at[i, dz, dx],
            recv_sem=part_recv.at[i, place[0], place[1]],
            device_id={"dp": dp_at(dz), "expert": ex_at(dx)},
            device_id_type=MESH,
        )

    def swap_copy(i, out_ref, in_ref):
        return pltpu.make_async_remote_copy(
            src_ref=out_ref,
            dst_ref=in_ref,
            send_sem=swap_send.at[i],
            recv_sem=swap_recv.at[i],
            device_id={"tensor": other_core},
            device_id_type=MESH,
        )

    def send_pages(i):
        for dz, dx in peers + [(0, 0)]:
            tenant = tenants[dp_at(dz) * ex_size + ex_at(dx)]
            for local in range(exp_dev):
                slot = table[me_ex * exp_dev + local, tenant]
                if i == 0:
                    page = all_in[local, slot]
                    rows = {0: page[:rank], 1: page[rank:]}
                else:
                    rows = {2: all_down[local, slot]}
                for kind, value in rows.items():
                    if (dz, dx) == (0, 0):
                        pages[me_dp, kind, me_ex, local] = value
                    else:
                        pages_out[dp_at(dz), ex_at(dx), kind, local] = value
            if (dz, dx) != (0, 0):
                page_copy(i, dz, dx, (me_dp, me_ex)).start()

    def project(i, rows):
        total = None
        for dz in [0] + dp_order[:-1]:
            d = dp_at(dz)
            for dx in range(ex_size):
                if (dz, dx) != (0, 0):
                    page_copy(i, dz, dx, (d, ex_at(dx))).wait_recv()
            page = pages[d, 0:2] if i == 0 else pages[d, 2]
            part = matmul(page.reshape(-1, piece), rows[d], LAST_LAST)
            total = part if total is None else total + part
        return total

    def send_parts(i, values, rows):
        for dz in dp_order:
            d = dp_at(dz)
            part = matmul(values, rows[d]).astype(BF16)
            if i == 0:
                parts_out[d, 0:2] = part.reshape(2, ex_size, exp_dev, rank, piece)
            else:
                parts_out[d, 2] = part.reshape(ex_size, exp_dev, rank, piece)
            for dx in range(ex_size):
                if (dz, dx) != (0, 0):
                    part_copy(i, dz, dx, (me_dp, me_ex)).start()

    small_loads[0].wait()
    small_loads[1].wait()
    load_in.wait()
    pl.semaphore_wait(barrier, len(peers) + 1)
    send_pages(0)
    load_down.wait()
    send_pages(1)

    for load in small_loads[2:] + tok_loads:
        load.wait()
    expert_of = lax.broadcasted_iota(jnp.int32, (wide, tok_dev), 0) // rank
    chosen = [route[k : k + 1, :] == expert_of for k in range(top)]
    weight = sum(jnp.where(chosen[k], weight_of[k : k + 1, :], 0.0) for k in range(top))
    pre = project(0, tok)
    sums_out[...] = pre
    swap_pre = swap_copy(0, sums_out, sums_in)
    swap_pre.start()
    for load in cot_loads:
        load.wait()
    swap_pre.wait_recv()
    pre = pre + sums_in[...]
    gate = pre[:wide]
    upv = pre[wide:]
    sig = jax.nn.sigmoid(gate)
    act = gate * sig
    hidden = (act * upv).astype(BF16).astype(F32)
    weighted = weight * hidden
    send_parts(1, weighted.astype(BF16), cot)

    proj = project(1, cot)
    proj_out[...] = proj
    swap_proj = swap_copy(1, proj_out, proj_in)
    swap_proj.start()
    swap_proj.wait_recv()
    proj = proj + proj_in[...]
    hgrad = weight * proj
    lowrank = jnp.concatenate(
        [hgrad * upv * sig * (1.0 + gate * (1.0 - sig)), hgrad * act], axis=0
    )
    send_parts(0, lowrank.astype(BF16), tok)
    own = pltpu.make_async_copy(
        parts_out.at[me_dp, :, me_ex], grad_parts.at[me_dp, me_ex], own_sem
    )
    own.start()

    weighted = weighted.T.astype(BF16)
    lowrank = lowrank.T.astype(BF16)
    outs = []
    for p in range(dp_size):
        adapted_v[p] = matmul(weighted, pages[p, 2].reshape(wide, piece)).astype(BF16)
        outs.append(
            pltpu.make_async_copy(adapted_v.at[p], adapted.at[:, columns(p)], out_sem.at[0, p])
        )
        outs[-1].start()
        grad_tokens_v[p] = matmul(lowrank, pages[p, 0:2].reshape(2 * wide, piece)).astype(BF16)
        outs.append(
            pltpu.make_async_copy(
                grad_tokens_v.at[p], grad_tokens.at[:, columns(p)], out_sem.at[1, p]
            )
        )
        outs[-1].start()
    product = hidden * proj
    for k in range(top):
        grad_weight_v[k : k + 1, :] = jnp.sum(
            jnp.where(chosen[k], product, 0.0), axis=0, keepdims=True
        )
    outs.append(pltpu.make_async_copy(grad_weight_v, grad_weight, out_sem.at[2, 0]))
    outs[-1].start()

    for out in outs:
        out.wait()
    swap_pre.wait_send()
    swap_proj.wait_send()
    own.wait()
    for i in range(2):
        for dz, dx in peers:
            page_copy(i, dz, dx, (me_dp, me_ex)).wait_send()
    for i in (1, 0):
        for dz, dx in peers:
            part_copy(i, dz, dx, (me_dp, me_ex)).wait_send()
            part_copy(i, dz, dx, (dp_at(dz), ex_at(dx))).wait_recv()


def scatter_kernel(
    sizes, slots,
    block_tenant, page_table, parts, adapted, grad_tokens, grad_weight,
    grad_in, grad_down, adapted_out, grad_tokens_out, grad_weight_out,
    tenants, table, parts_v, adapted_v, grad_tokens_v, grad_weight_v,
    small_sem, parts_sem, enter_sem, leave_sem,
):
    dp_size, ex_size, exp_dev, rank = sizes
    local = pl.program_id(0)
    chunk = pl.program_id(1)
    loads = [
        pltpu.make_async_copy(block_tenant, tenants, small_sem.at[0]),
        pltpu.make_async_copy(page_table, table, small_sem.at[1]),
        pltpu.make_async_copy(parts, parts_v, parts_sem),
    ]
    passed = [
        (adapted, adapted_v, adapted_out),
        (grad_tokens, grad_tokens_v, grad_tokens_out),
        (grad_weight, grad_weight_v, grad_weight_out),
    ]
    enter = [
        pltpu.make_async_copy(source, held, enter_sem.at[i])
        for i, (source, held, _) in enumerate(passed)
    ]
    leave = [
        pltpu.make_async_copy(held, target, leave_sem.at[i])
        for i, (_, held, target) in enumerate(passed)
    ]
    step = local * pl.num_programs(1) + chunk

    @pl.when(step == 0)
    def _():
        for load in loads + enter:
            load.start()

    grad_in[...] = jnp.zeros_like(grad_in)
    grad_down[...] = jnp.zeros_like(grad_down)

    @pl.when(step == 0)
    def _():
        for load in loads:
            load.wait()

    @pl.when(step == 1)
    def _():
        for load in enter:
            load.wait()
        for store in leave:
            store.start()

    expert = lax.axis_index("expert") * exp_dev + local
    for d in range(dp_size):
        for x in range(ex_size):
            place = table[expert, tenants[d * ex_size + x]] - chunk * slots

            @pl.when((place >= 0) & (place < slots))
            def _():
                grad_in[0, place, :rank] += parts_v[d, x, 0, local].astype(F32)
                grad_in[0, place, rank:] += parts_v[d, x, 1, local].astype(F32)
                grad_down[0, place] += parts_v[d, x, 2, local].astype(F32)

    @pl.when(step == pl.num_programs(0) * pl.num_programs(1) - 1)
    def _():
        for store in leave:
            store.wait()


def paged(
    tokens, routes, route_weight, block_tenant, page_table, adapter_in, adapter_down, upstream
):
    tok_dev, half = tokens.shape
    top = routes.shape[1]
    exp_dev, tenants, _, piece = adapter_in.shape
    rank = adapter_down.shape[2]
    dp_size = lax.axis_size("dp")
    ex_size = lax.axis_size("expert")
    wide = ex_size * exp_dev * rank
    sizes = (dp_size, ex_size, exp_dev, rank, piece, tok_dev, top)
    any_spec = pl.BlockSpec(memory_space=pl.ANY)
    dma = pltpu.SemaphoreType.DMA
    parts_shape = (dp_size, ex_size, 3, exp_dev, rank, piece)
    weight_shape = jax.ShapeDtypeStruct((top, tok_dev), F32)
    rows_shape = jax.ShapeDtypeStruct((tok_dev, half), BF16)
    small_scratch = [
        pltpu.SMEM(block_tenant.shape, jnp.int32),
        pltpu.SMEM(page_table.shape, jnp.int32),
    ]
    adapted, grad_tokens, grad_weight, parts = pl.pallas_call(
        functools.partial(adapter_kernel, sizes),
        out_shape=(
            rows_shape,
            rows_shape,
            weight_shape,
            jax.ShapeDtypeStruct(parts_shape, BF16),
        ),
        in_specs=[any_spec] * 8,
        out_specs=(any_spec,) * 4,
        scratch_shapes=small_scratch
        + [
            pltpu.VMEM((top, tok_dev), jnp.int32),
            pltpu.VMEM((top, tok_dev), F32),
            pltpu.VMEM(adapter_in.shape, BF16),
            pltpu.VMEM(adapter_down.shape, BF16),
            pltpu.VMEM((dp_size, tok_dev, piece), BF16),
            pltpu.VMEM((dp_size, tok_dev, piece), BF16),
            pltpu.VMEM(parts_shape, BF16),
            pltpu.VMEM((dp_size, 3, ex_size, exp_dev, rank, piece), BF16),
            pltpu.VMEM((2 * wide, tok_dev), F32),
            pltpu.VMEM((2 * wide, tok_dev), F32),
            pltpu.VMEM((wide, tok_dev), F32),
            pltpu.VMEM((wide, tok_dev), F32),
            pltpu.VMEM((dp_size, 3, ex_size, exp_dev, rank, piece), BF16),
            pltpu.VMEM((dp_size, tok_dev, piece), BF16),
            pltpu.VMEM((dp_size, tok_dev, piece), BF16),
            pltpu.VMEM((top, tok_dev), F32),
            dma((4,)),
            dma((2,)),
            dma((2, dp_size)),
            dma((2, dp_size, ex_size)),
            dma((2, dp_size, ex_size)),
            dma((2,)),
            dma((2,)),
            dma((2, dp_size, ex_size)),
            dma((2, dp_size, ex_size)),
            dma,
            dma((3, dp_size)),
        ],
        compiler_params=pltpu.CompilerParams(
            collective_id=0, has_side_effects=True, vmem_limit_bytes=60 << 20
        ),
    )(
        block_tenant, page_table, routes.T, route_weight.T,
        tokens, upstream, adapter_in, adapter_down,
    )
    slots = 8
    grad_in, grad_down, adapted, grad_tokens, grad_weight = pl.pallas_call(
        functools.partial(scatter_kernel, (dp_size, ex_size, exp_dev, rank), slots),
        grid=(exp_dev, tenants // slots),
        out_shape=(
            jax.ShapeDtypeStruct((exp_dev, tenants, 2 * rank, piece), F32),
            jax.ShapeDtypeStruct((exp_dev, tenants, rank, piece), F32),
            rows_shape,
            rows_shape,
            weight_shape,
        ),
        in_specs=[any_spec] * 6,
        out_specs=(
            pl.BlockSpec((1, slots, 2 * rank, piece), lambda i, j: (i, j, 0, 0)),
            pl.BlockSpec((1, slots, rank, piece), lambda i, j: (i, j, 0, 0)),
            any_spec,
            any_spec,
            any_spec,
        ),
        scratch_shapes=small_scratch
        + [
            pltpu.VMEM(parts_shape, BF16),
            pltpu.VMEM((tok_dev, half), BF16),
            pltpu.VMEM((tok_dev, half), BF16),
            pltpu.VMEM((top, tok_dev), F32),
            dma((2,)),
            dma,
            dma((3,)),
            dma((3,)),
        ],
        compiler_params=pltpu.CompilerParams(vmem_limit_bytes=60 << 20),
    )(block_tenant, page_table, parts, adapted, grad_tokens, grad_weight)
    return (adapted, grad_tokens, grad_weight.T, grad_in, grad_down)


def feature_sum(partial_value):
    return lax.psum(partial_value, "tensor")


def swap_blocks(block):
    return lax.all_to_all(block, "expert", split_axis=0, concat_axis=0, tiled=True)


def routed(
    tokens, routes, route_weight, block_tenant, page_table, adapter_in, adapter_down, upstream
):
    tok_dev, half = tokens.shape
    top = routes.shape[1]
    exp_dev = adapter_in.shape[0]
    tenants = adapter_in.shape[1]
    rank = adapter_down.shape[2]
    piece = adapter_in.shape[3]
    dp_size = lax.axis_size("dp")
    ex_size = lax.axis_size("expert")
    experts = exp_dev * ex_size
    column = lax.axis_index("expert")
    tenant_grid = block_tenant.reshape(dp_size, ex_size)
    local_table = lax.dynamic_slice_in_dim(page_table, column * exp_dev, exp_dev, 0)
    wanted = local_table[:, tenant_grid]
    flat_in = adapter_in.reshape(exp_dev, tenants, 2 * rank * piece)
    flat_down = adapter_down.reshape(exp_dev, tenants, rank * piece)
    send_in = jnp.stack([flat_in[local][wanted[local]] for local in range(exp_dev)], axis=1)
    send_down = jnp.stack([flat_down[local][wanted[local]] for local in range(exp_dev)], axis=1)
    got_in, got_down = (
        lax.all_to_all(send_in, "dp", split_axis=0, concat_axis=0, tiled=True),
        lax.all_to_all(send_down, "dp", split_axis=0, concat_axis=0, tiled=True),
    )
    page_in = (
        got_in.reshape(dp_size, exp_dev, ex_size, 2 * rank, piece)
        .transpose(1, 2, 3, 0, 4)
        .reshape(exp_dev, ex_size, 2 * rank, half)
    )
    page_down = (
        got_down.reshape(dp_size, exp_dev, ex_size, rank, piece)
        .transpose(1, 2, 3, 0, 4)
        .reshape(exp_dev, ex_size, rank, half)
    )
    scaled = (route_weight[:, :, None] * upstream[:, None, :].astype(jnp.float32)).astype(
        jnp.bfloat16
    )
    cap = 5 * tok_dev * top // (4 * experts)
    slot_count = experts * cap
    flat_routes = routes.reshape(-1)
    hits = (flat_routes[:, None] == jnp.arange(experts, dtype=jnp.int32)[None, :]).astype(jnp.int32)
    position = jnp.sum((jnp.cumsum(hits, axis=0) - 1) * hits, axis=1)
    slot = flat_routes * cap + position
    placing = (slot[None, :] == jnp.arange(slot_count, dtype=jnp.int32)[:, None]).astype(
        jnp.bfloat16
    )
    placing_tok = jnp.sum(placing.reshape(slot_count, tok_dev, top), axis=2)
    rows_send = jnp.dot(placing_tok, tokens, preferred_element_type=jnp.float32).astype(
        jnp.bfloat16
    )
    arrived = swap_blocks(rows_send).reshape(ex_size, exp_dev, cap, half)
    pre = feature_sum(
        jnp.einsum("kecd,ekrd->kecr", arrived, page_in, preferred_element_type=jnp.float32)
    )
    gate = pre[..., :rank]
    upv = pre[..., rank:]
    sig = jax.nn.sigmoid(gate)
    act = gate * sig
    hidden = (act * upv).astype(jnp.bfloat16)
    branch = jnp.einsum(
        "kecr,ekrd->kecd", hidden, page_down, preferred_element_type=jnp.float32
    ).astype(jnp.bfloat16)
    returned = swap_blocks(branch.reshape(slot_count, half))
    picked = returned[slot].reshape(tok_dev, top, half)
    adapted = jnp.sum(route_weight[:, :, None] * picked.astype(jnp.float32), axis=1).astype(
        jnp.bfloat16
    )
    grad_weight = feature_sum(
        jnp.einsum("td,tkd->tk", upstream, picked, preferred_element_type=jnp.float32)
    )
    cot_send = jnp.dot(
        placing, scaled.reshape(tok_dev * top, half), preferred_element_type=jnp.float32
    ).astype(jnp.bfloat16)
    cot_blocks = swap_blocks(cot_send).reshape(ex_size, exp_dev, cap, half)
    hgrad = feature_sum(
        jnp.einsum("kecd,ekrd->kecr", cot_blocks, page_down, preferred_element_type=jnp.float32)
    )
    lowrank = jnp.concatenate(
        [hgrad * upv * sig * (1.0 + gate * (1.0 - sig)), hgrad * act], axis=3
    ).astype(jnp.bfloat16)
    input_grad = jnp.einsum(
        "kecr,ekrd->kecd", lowrank, page_in, preferred_element_type=jnp.float32
    ).astype(jnp.bfloat16)
    req_in = jnp.einsum("kecr,kecd->ekrd", lowrank, arrived, preferred_element_type=jnp.float32)
    req_down = jnp.einsum("kecr,kecd->ekrd", hidden, cot_blocks, preferred_element_type=jnp.float32)
    grad_back = swap_blocks(input_grad.reshape(slot_count, half))
    grad_tokens = jnp.sum(
        grad_back[slot].reshape(tok_dev, top, half).astype(jnp.float32), axis=1
    ).astype(jnp.bfloat16)
    out_in = (
        req_in.reshape(exp_dev, ex_size, 2 * rank, dp_size, piece)
        .transpose(3, 0, 1, 2, 4)
        .reshape(dp_size, exp_dev, ex_size, 2 * rank * piece)
    )
    out_down = (
        req_down.reshape(exp_dev, ex_size, rank, dp_size, piece)
        .transpose(3, 0, 1, 2, 4)
        .reshape(dp_size, exp_dev, ex_size, rank * piece)
    )
    recv_in, recv_down = (
        lax.all_to_all(out_in, "dp", split_axis=0, concat_axis=0, tiled=True),
        lax.all_to_all(out_down, "dp", split_axis=0, concat_axis=0, tiled=True),
    )
    sums_in = []
    sums_down = []
    for local in range(exp_dev):
        owners = wanted[local].reshape(-1)
        sums_in.append(
            jnp.zeros((tenants, 2 * rank * piece), jnp.float32)
            .at[owners]
            .add(recv_in[:, local].reshape(dp_size * ex_size, -1))
        )
        sums_down.append(
            jnp.zeros((tenants, rank * piece), jnp.float32)
            .at[owners]
            .add(recv_down[:, local].reshape(dp_size * ex_size, -1))
        )
    grad_in = jnp.stack(sums_in, axis=0).reshape(exp_dev, tenants, 2 * rank, piece)
    grad_down = jnp.stack(sums_down, axis=0).reshape(exp_dev, tenants, rank, piece)
    return (adapted, grad_tokens, grad_weight, grad_in, grad_down)


def shards(*arrays):
    rank, piece = arrays[6].shape[2:]
    whole_tiles = piece % 128 == 0 and rank % 16 == 0 and lax.axis_size("tensor") == 2
    return paged(*arrays) if whole_tiles else routed(*arrays)


def solution(mesh):
    return jax.shard_map(
        shards,
        mesh=mesh,
        in_specs=(
            P(("groups", "dp", "expert"), "tensor"),
            P(("groups", "dp", "expert"), None),
            P(("groups", "dp", "expert"), None),
            P("groups"),
            P(),
            P("expert", None, None, ("tensor", "dp")),
            P("expert", None, None, ("tensor", "dp")),
            P(("groups", "dp", "expert"), "tensor"),
        ),
        out_specs=(
            P(("groups", "dp", "expert"), "tensor"),
            P(("groups", "dp", "expert"), "tensor"),
            P(("groups", "dp", "expert"), None),
            P(("groups", "expert"), None, None, ("tensor", "dp")),
            P(("groups", "expert"), None, None, ("tensor", "dp")),
        ),
        check_vma=False,
    )
```

```python
import functools

import jax
import jax.numpy as jnp
from jax import lax
from jax.experimental import pallas as pl
from jax.experimental.pallas import tpu as pltpu
from jax.sharding import PartitionSpec as P

BF16 = jnp.bfloat16
F32 = jnp.float32
MESH = pl.DeviceIdType.MESH
LAST_LAST = (((1,), (1,)), ((), ()))
PLAIN = (((1,), (0,)), ((), ()))


def matmul(left, right, dims=PLAIN):
    return lax.dot_general(left, right, dims, preferred_element_type=F32)


def step_order(size):
    half = size // 2
    return list(range(half, size)) + list(range(1, half)) + [0]


def adapter_kernel(
    sizes,
    block_tenant, page_table, routes, weights, tokens, upstream, adapter_in, adapter_down,
    adapted, grad_tokens, grad_weight, grad_parts,
    tenants, table, route, weight_of,
    all_in, all_down, tok, cot, pages_out, pages, sums_out, sums_in, proj_out, proj_in,
    parts_out, adapted_v, grad_tokens_v, grad_weight_v,
    small_sem, load_sem, token_sem, page_send, page_recv, swap_send, swap_recv,
    part_send, part_recv, own_sem, out_sem,
):
    dp_size, ex_size, exp_dev, rank, piece, tok_dev, top = sizes
    wide = ex_size * exp_dev * rank
    kinds = (pl.ds(0, 2), pl.ds(2, 1))
    me_dp = lax.axis_index("dp")
    me_ex = lax.axis_index("expert")
    other_core = lax.rem(lax.axis_index("tensor") + 1, 2)
    dp_order = step_order(dp_size)
    peers = [(dz, dx) for dz in dp_order for dx in reversed(range(ex_size)) if (dz, dx) != (0, 0)]

    def dp_at(dz):
        half = dp_size // 2
        side = lax.rem(me_dp // half + dz // half, 2)
        return side * half + lax.rem(me_dp + dz, half)

    def ex_at(dx):
        return lax.rem(me_ex + dx, ex_size)

    def columns(p):
        return pl.ds(p * piece, piece)

    barrier = pltpu.get_barrier_semaphore()
    for dz, dx in peers:
        pl.semaphore_signal(
            barrier, inc=1, device_id={"dp": dp_at(dz), "expert": ex_at(dx)}, device_id_type=MESH
        )
    pl.semaphore_signal(barrier, inc=1, device_id={"tensor": other_core}, device_id_type=MESH)

    small_loads = [
        pltpu.make_async_copy(source, target, small_sem.at[i])
        for i, (source, target) in enumerate(
            [(block_tenant, tenants), (page_table, table), (routes, route), (weights, weight_of)]
        )
    ]
    load_in = pltpu.make_async_copy(adapter_in, all_in, load_sem.at[0])
    load_down = pltpu.make_async_copy(adapter_down, all_down, load_sem.at[1])
    tok_loads = [
        pltpu.make_async_copy(tokens.at[:, columns(p)], tok.at[p], token_sem.at[0, p])
        for p in range(dp_size)
    ]
    cot_loads = [
        pltpu.make_async_copy(upstream.at[:, columns(p)], cot.at[p], token_sem.at[1, p])
        for p in range(dp_size)
    ]
    for load in small_loads + [load_in, load_down]:
        load.start()

    def page_copy(i, dz, dx, place):
        return pltpu.make_async_remote_copy(
            src_ref=pages_out.at[dp_at(dz), ex_at(dx), kinds[i]],
            dst_ref=pages.at[place[0], kinds[i], place[1]],
            send_sem=page_send.at[i, dz, dx],
            recv_sem=page_recv.at[i, place[0], place[1]],
            device_id={"dp": dp_at(dz), "expert": ex_at(dx)},
            device_id_type=MESH,
        )

    def part_copy(i, dz, dx, place):
        return pltpu.make_async_remote_copy(
            src_ref=parts_out.at[dp_at(dz), kinds[i], ex_at(dx)],
            dst_ref=grad_parts.at[place[0], place[1], kinds[i]],
            send_sem=part_send.at[i, dz, dx],
            recv_sem=part_recv.at[i, place[0], place[1]],
            device_id={"dp": dp_at(dz), "expert": ex_at(dx)},
            device_id_type=MESH,
        )

    def swap_copy(i, out_ref, in_ref):
        return pltpu.make_async_remote_copy(
            src_ref=out_ref,
            dst_ref=in_ref,
            send_sem=swap_send.at[i],
            recv_sem=swap_recv.at[i],
            device_id={"tensor": other_core},
            device_id_type=MESH,
        )

    def send_pages(i):
        for dz, dx in peers + [(0, 0)]:
            tenant = tenants[dp_at(dz) * ex_size + ex_at(dx)]
            for local in range(exp_dev):
                slot = table[me_ex * exp_dev + local, tenant]
                if i == 0:
                    page = all_in[local, slot]
                    rows = {0: page[:rank], 1: page[rank:]}
                else:
                    rows = {2: all_down[local, slot]}
                for kind, value in rows.items():
                    if (dz, dx) == (0, 0):
                        pages[me_dp, kind, me_ex, local] = value
                    else:
                        pages_out[dp_at(dz), ex_at(dx), kind, local] = value
            if (dz, dx) != (0, 0):
                page_copy(i, dz, dx, (me_dp, me_ex)).start()

    def project(i, rows):
        total = None
        for dz in [0] + dp_order[:-1]:
            d = dp_at(dz)
            for dx in reversed(range(ex_size)):
                if (dz, dx) != (0, 0):
                    page_copy(i, dz, dx, (d, ex_at(dx))).wait_recv()
            page = pages[d, 0:2] if i == 0 else pages[d, 2]
            part = matmul(page.reshape(-1, piece), rows[d], LAST_LAST)
            total = part if total is None else total + part
        return total

    def send_parts(i, values, rows):
        for dz in dp_order:
            d = dp_at(dz)
            part = matmul(values, rows[d]).astype(BF16)
            if i == 0:
                parts_out[d, 0:2] = part.reshape(2, ex_size, exp_dev, rank, piece)
            else:
                parts_out[d, 2] = part.reshape(ex_size, exp_dev, rank, piece)
            for dx in reversed(range(ex_size)):
                if (dz, dx) != (0, 0):
                    part_copy(i, dz, dx, (me_dp, me_ex)).start()

    small_loads[0].wait()
    small_loads[1].wait()
    load_in.wait()
    pl.semaphore_wait(barrier, len(peers) + 1)
    send_pages(0)
    load_down.wait()
    for load in tok_loads + cot_loads:
        load.start()
    send_pages(1)

    for load in small_loads[2:] + tok_loads:
        load.wait()
    expert_of = lax.broadcasted_iota(jnp.int32, (wide, tok_dev), 0) // rank
    chosen = [route[k : k + 1, :] == expert_of for k in range(top)]
    weight = sum(jnp.where(chosen[k], weight_of[k : k + 1, :], 0.0) for k in range(top))
    pre = project(0, tok)
    sums_out[...] = pre
    swap_pre = swap_copy(0, sums_out, sums_in)
    swap_pre.start()
    for load in cot_loads:
        load.wait()
    swap_pre.wait_recv()
    pre = pre + sums_in[...]
    gate = pre[:wide]
    upv = pre[wide:]
    sig = jax.nn.sigmoid(gate)
    act = gate * sig
    hidden = (act * upv).astype(BF16).astype(F32)
    weighted = weight * hidden
    send_parts(1, weighted.astype(BF16), cot)

    proj = project(1, cot)
    proj_out[...] = proj
    swap_proj = swap_copy(1, proj_out, proj_in)
    swap_proj.start()
    swap_proj.wait_recv()
    proj = proj + proj_in[...]
    hgrad = weight * proj
    lowrank = jnp.concatenate(
        [hgrad * upv * sig * (1.0 + gate * (1.0 - sig)), hgrad * act], axis=0
    )
    send_parts(0, lowrank.astype(BF16), tok)
    own = pltpu.make_async_copy(
        parts_out.at[me_dp, :, me_ex], grad_parts.at[me_dp, me_ex], own_sem
    )
    own.start()

    weighted = weighted.T.astype(BF16)
    lowrank = lowrank.T.astype(BF16)
    outs = []
    for p in range(dp_size):
        adapted_v[p] = matmul(weighted, pages[p, 2].reshape(wide, piece)).astype(BF16)
        outs.append(
            pltpu.make_async_copy(adapted_v.at[p], adapted.at[:, columns(p)], out_sem.at[0, p])
        )
        outs[-1].start()
        grad_tokens_v[p] = matmul(lowrank, pages[p, 0:2].reshape(2 * wide, piece)).astype(BF16)
        outs.append(
            pltpu.make_async_copy(
                grad_tokens_v.at[p], grad_tokens.at[:, columns(p)], out_sem.at[1, p]
            )
        )
        outs[-1].start()
    product = hidden * proj
    for k in range(top):
        grad_weight_v[k : k + 1, :] = jnp.sum(
            jnp.where(chosen[k], product, 0.0), axis=0, keepdims=True
        )
    outs.append(pltpu.make_async_copy(grad_weight_v, grad_weight, out_sem.at[2, 0]))
    outs[-1].start()

    for out in outs:
        out.wait()
    swap_pre.wait_send()
    swap_proj.wait_send()
    own.wait()
    for i in range(2):
        for dz, dx in peers:
            page_copy(i, dz, dx, (me_dp, me_ex)).wait_send()
    for i in (1, 0):
        for dz, dx in peers:
            part_copy(i, dz, dx, (me_dp, me_ex)).wait_send()
            part_copy(i, dz, dx, (dp_at(dz), ex_at(dx))).wait_recv()


def scatter_kernel(
    sizes,
    block_tenant, page_table, parts, adapted, grad_tokens, grad_weight,
    grad_in, grad_down, adapted_out, grad_tokens_out, grad_weight_out,
    tenants, table, parts_v, adapted_v, grad_tokens_v, grad_weight_v,
    zeros, total_in, total_down,
    small_sem, parts_sem, enter_sem, leave_sem, zero_sem, total_sem,
):
    dp_size, ex_size, exp_dev, rank, slots = sizes
    blocks = dp_size * ex_size
    chunk = zeros.shape[0]
    me_ex = lax.axis_index("expert")
    loads = [
        pltpu.make_async_copy(block_tenant, tenants, small_sem.at[0]),
        pltpu.make_async_copy(page_table, table, small_sem.at[1]),
        pltpu.make_async_copy(parts, parts_v, parts_sem),
    ]
    passed = [
        (adapted, adapted_v, adapted_out),
        (grad_tokens, grad_tokens_v, grad_tokens_out),
        (grad_weight, grad_weight_v, grad_weight_out),
    ]
    enter = [
        pltpu.make_async_copy(source, held, enter_sem.at[i])
        for i, (source, held, _) in enumerate(passed)
    ]
    leave = [
        pltpu.make_async_copy(held, target, leave_sem.at[i])
        for i, (_, held, target) in enumerate(passed)
    ]
    for load in loads + enter:
        load.start()

    zeros[...] = jnp.zeros_like(zeros)
    clears = []
    for local in range(exp_dev):
        for i, start in enumerate(range(0, slots, chunk)):
            place = pl.ds(start, chunk)
            clears.append(
                [
                    pltpu.make_async_copy(
                        zeros, grad_in.at[local, place], zero_sem.at[local, i, 0]
                    ),
                    pltpu.make_async_copy(
                        zeros.at[:, :rank], grad_down.at[local, place], zero_sem.at[local, i, 1]
                    ),
                ]
            )
            for clear in clears[-1]:
                clear.start()

    for load in loads:
        load.wait()
    tenant = [tenants[b] for b in range(blocks)]
    leads = []
    for b in range(blocks):
        first = jnp.bool_(True)
        for other in range(b):
            first = first & (tenant[other] != tenant[b])
        leads.append(first)
        part = parts_v[b // ex_size, b % ex_size].astype(F32)
        total_in[b, :, :rank] = part[0]
        total_in[b, :, rank:] = part[1]
        total_down[b] = part[2]
    for b in range(blocks):
        for later in range(b + 1, blocks):

            @pl.when(leads[b] & (tenant[later] == tenant[b]))
            def _():
                part = parts_v[later // ex_size, later % ex_size].astype(F32)
                total_in[b, :, :rank] += part[0]
                total_in[b, :, rank:] += part[1]
                total_down[b] += part[2]

    for load in enter:
        load.wait()
    for store in leave:
        store.start()

    def stores(local, b):
        slot = table[me_ex * exp_dev + local, tenant[b]]
        return [
            pltpu.make_async_copy(
                total_in.at[b, local], grad_in.at[local, slot], total_sem.at[local, b, 0]
            ),
            pltpu.make_async_copy(
                total_down.at[b, local], grad_down.at[local, slot], total_sem.at[local, b, 1]
            ),
        ]

    per_expert = slots // chunk
    for local in range(exp_dev):
        for pair in clears[local * per_expert : (local + 1) * per_expert]:
            for clear in pair:
                clear.wait()
        for b in range(blocks):

            @pl.when(leads[b])
            def _():
                for store in stores(local, b):
                    store.start()

    for local in range(exp_dev):
        for b in range(blocks):

            @pl.when(leads[b])
            def _():
                for store in stores(local, b):
                    store.wait()

    for store in leave:
        store.wait()


def paged(
    tokens, routes, route_weight, block_tenant, page_table, adapter_in, adapter_down, upstream
):
    tok_dev, half = tokens.shape
    top = routes.shape[1]
    exp_dev, tenants, _, piece = adapter_in.shape
    rank = adapter_down.shape[2]
    dp_size = lax.axis_size("dp")
    ex_size = lax.axis_size("expert")
    wide = ex_size * exp_dev * rank
    sizes = (dp_size, ex_size, exp_dev, rank, piece, tok_dev, top)
    any_spec = pl.BlockSpec(memory_space=pl.ANY)
    dma = pltpu.SemaphoreType.DMA
    parts_shape = (dp_size, ex_size, 3, exp_dev, rank, piece)
    weight_shape = jax.ShapeDtypeStruct((top, tok_dev), F32)
    rows_shape = jax.ShapeDtypeStruct((tok_dev, half), BF16)
    small_scratch = [
        pltpu.SMEM(block_tenant.shape, jnp.int32),
        pltpu.SMEM(page_table.shape, jnp.int32),
    ]
    adapted, grad_tokens, grad_weight, parts = pl.pallas_call(
        functools.partial(adapter_kernel, sizes),
        out_shape=(
            rows_shape,
            rows_shape,
            weight_shape,
            jax.ShapeDtypeStruct(parts_shape, BF16),
        ),
        in_specs=[any_spec] * 8,
        out_specs=(any_spec,) * 4,
        scratch_shapes=small_scratch
        + [
            pltpu.VMEM((top, tok_dev), jnp.int32),
            pltpu.VMEM((top, tok_dev), F32),
            pltpu.VMEM(adapter_in.shape, BF16),
            pltpu.VMEM(adapter_down.shape, BF16),
            pltpu.VMEM((dp_size, tok_dev, piece), BF16),
            pltpu.VMEM((dp_size, tok_dev, piece), BF16),
            pltpu.VMEM(parts_shape, BF16),
            pltpu.VMEM((dp_size, 3, ex_size, exp_dev, rank, piece), BF16),
            pltpu.VMEM((2 * wide, tok_dev), F32),
            pltpu.VMEM((2 * wide, tok_dev), F32),
            pltpu.VMEM((wide, tok_dev), F32),
            pltpu.VMEM((wide, tok_dev), F32),
            pltpu.VMEM((dp_size, 3, ex_size, exp_dev, rank, piece), BF16),
            pltpu.VMEM((dp_size, tok_dev, piece), BF16),
            pltpu.VMEM((dp_size, tok_dev, piece), BF16),
            pltpu.VMEM((top, tok_dev), F32),
            dma((4,)),
            dma((2,)),
            dma((2, dp_size)),
            dma((2, dp_size, ex_size)),
            dma((2, dp_size, ex_size)),
            dma((2,)),
            dma((2,)),
            dma((2, dp_size, ex_size)),
            dma((2, dp_size, ex_size)),
            dma,
            dma((3, dp_size)),
        ],
        compiler_params=pltpu.CompilerParams(
            collective_id=0, has_side_effects=True, vmem_limit_bytes=60 << 20
        ),
    )(
        block_tenant, page_table, routes.T, route_weight.T,
        tokens, upstream, adapter_in, adapter_down,
    )
    blocks = dp_size * ex_size
    chunk = 8
    grad_in, grad_down, adapted, grad_tokens, grad_weight = pl.pallas_call(
        functools.partial(scatter_kernel, (dp_size, ex_size, exp_dev, rank, tenants)),
        out_shape=(
            jax.ShapeDtypeStruct((exp_dev, tenants, 2 * rank, piece), F32),
            jax.ShapeDtypeStruct((exp_dev, tenants, rank, piece), F32),
            rows_shape,
            rows_shape,
            weight_shape,
        ),
        in_specs=[any_spec] * 6,
        out_specs=(any_spec,) * 5,
        scratch_shapes=small_scratch
        + [
            pltpu.VMEM(parts_shape, BF16),
            pltpu.VMEM((tok_dev, half), BF16),
            pltpu.VMEM((tok_dev, half), BF16),
            pltpu.VMEM((top, tok_dev), F32),
            pltpu.VMEM((chunk, 2 * rank, piece), F32),
            pltpu.VMEM((blocks, exp_dev, 2 * rank, piece), F32),
            pltpu.VMEM((blocks, exp_dev, rank, piece), F32),
            dma((2,)),
            dma,
            dma((3,)),
            dma((3,)),
            dma((exp_dev, tenants // chunk, 2)),
            dma((exp_dev, blocks, 2)),
        ],
        compiler_params=pltpu.CompilerParams(vmem_limit_bytes=60 << 20),
    )(block_tenant, page_table, parts, adapted, grad_tokens, grad_weight)
    return (adapted, grad_tokens, grad_weight.T, grad_in, grad_down)


def feature_sum(partial_value):
    return lax.psum(partial_value, "tensor")


def swap_blocks(block):
    return lax.all_to_all(block, "expert", split_axis=0, concat_axis=0, tiled=True)


def routed(
    tokens, routes, route_weight, block_tenant, page_table, adapter_in, adapter_down, upstream
):
    tok_dev, half = tokens.shape
    top = routes.shape[1]
    exp_dev = adapter_in.shape[0]
    tenants = adapter_in.shape[1]
    rank = adapter_down.shape[2]
    piece = adapter_in.shape[3]
    dp_size = lax.axis_size("dp")
    ex_size = lax.axis_size("expert")
    experts = exp_dev * ex_size
    column = lax.axis_index("expert")
    tenant_grid = block_tenant.reshape(dp_size, ex_size)
    local_table = lax.dynamic_slice_in_dim(page_table, column * exp_dev, exp_dev, 0)
    wanted = local_table[:, tenant_grid]
    flat_in = adapter_in.reshape(exp_dev, tenants, 2 * rank * piece)
    flat_down = adapter_down.reshape(exp_dev, tenants, rank * piece)
    send_in = jnp.stack([flat_in[local][wanted[local]] for local in range(exp_dev)], axis=1)
    send_down = jnp.stack([flat_down[local][wanted[local]] for local in range(exp_dev)], axis=1)
    got_in, got_down = (
        lax.all_to_all(send_in, "dp", split_axis=0, concat_axis=0, tiled=True),
        lax.all_to_all(send_down, "dp", split_axis=0, concat_axis=0, tiled=True),
    )
    page_in = (
        got_in.reshape(dp_size, exp_dev, ex_size, 2 * rank, piece)
        .transpose(1, 2, 3, 0, 4)
        .reshape(exp_dev, ex_size, 2 * rank, half)
    )
    page_down = (
        got_down.reshape(dp_size, exp_dev, ex_size, rank, piece)
        .transpose(1, 2, 3, 0, 4)
        .reshape(exp_dev, ex_size, rank, half)
    )
    scaled = (route_weight[:, :, None] * upstream[:, None, :].astype(jnp.float32)).astype(
        jnp.bfloat16
    )
    cap = 5 * tok_dev * top // (4 * experts)
    slot_count = experts * cap
    flat_routes = routes.reshape(-1)
    hits = (flat_routes[:, None] == jnp.arange(experts, dtype=jnp.int32)[None, :]).astype(jnp.int32)
    position = jnp.sum((jnp.cumsum(hits, axis=0) - 1) * hits, axis=1)
    slot = flat_routes * cap + position
    placing = (slot[None, :] == jnp.arange(slot_count, dtype=jnp.int32)[:, None]).astype(
        jnp.bfloat16
    )
    placing_tok = jnp.sum(placing.reshape(slot_count, tok_dev, top), axis=2)
    rows_send = jnp.dot(placing_tok, tokens, preferred_element_type=jnp.float32).astype(
        jnp.bfloat16
    )
    arrived = swap_blocks(rows_send).reshape(ex_size, exp_dev, cap, half)
    pre = feature_sum(
        jnp.einsum("kecd,ekrd->kecr", arrived, page_in, preferred_element_type=jnp.float32)
    )
    gate = pre[..., :rank]
    upv = pre[..., rank:]
    sig = jax.nn.sigmoid(gate)
    act = gate * sig
    hidden = (act * upv).astype(jnp.bfloat16)
    branch = jnp.einsum(
        "kecr,ekrd->kecd", hidden, page_down, preferred_element_type=jnp.float32
    ).astype(jnp.bfloat16)
    returned = swap_blocks(branch.reshape(slot_count, half))
    picked = returned[slot].reshape(tok_dev, top, half)
    adapted = jnp.sum(route_weight[:, :, None] * picked.astype(jnp.float32), axis=1).astype(
        jnp.bfloat16
    )
    grad_weight = feature_sum(
        jnp.einsum("td,tkd->tk", upstream, picked, preferred_element_type=jnp.float32)
    )
    cot_send = jnp.dot(
        placing, scaled.reshape(tok_dev * top, half), preferred_element_type=jnp.float32
    ).astype(jnp.bfloat16)
    cot_blocks = swap_blocks(cot_send).reshape(ex_size, exp_dev, cap, half)
    hgrad = feature_sum(
        jnp.einsum("kecd,ekrd->kecr", cot_blocks, page_down, preferred_element_type=jnp.float32)
    )
    lowrank = jnp.concatenate(
        [hgrad * upv * sig * (1.0 + gate * (1.0 - sig)), hgrad * act], axis=3
    ).astype(jnp.bfloat16)
    input_grad = jnp.einsum(
        "kecr,ekrd->kecd", lowrank, page_in, preferred_element_type=jnp.float32
    ).astype(jnp.bfloat16)
    req_in = jnp.einsum("kecr,kecd->ekrd", lowrank, arrived, preferred_element_type=jnp.float32)
    req_down = jnp.einsum("kecr,kecd->ekrd", hidden, cot_blocks, preferred_element_type=jnp.float32)
    grad_back = swap_blocks(input_grad.reshape(slot_count, half))
    grad_tokens = jnp.sum(
        grad_back[slot].reshape(tok_dev, top, half).astype(jnp.float32), axis=1
    ).astype(jnp.bfloat16)
    out_in = (
        req_in.reshape(exp_dev, ex_size, 2 * rank, dp_size, piece)
        .transpose(3, 0, 1, 2, 4)
        .reshape(dp_size, exp_dev, ex_size, 2 * rank * piece)
    )
    out_down = (
        req_down.reshape(exp_dev, ex_size, rank, dp_size, piece)
        .transpose(3, 0, 1, 2, 4)
        .reshape(dp_size, exp_dev, ex_size, rank * piece)
    )
    recv_in, recv_down = (
        lax.all_to_all(out_in, "dp", split_axis=0, concat_axis=0, tiled=True),
        lax.all_to_all(out_down, "dp", split_axis=0, concat_axis=0, tiled=True),
    )
    sums_in = []
    sums_down = []
    for local in range(exp_dev):
        owners = wanted[local].reshape(-1)
        sums_in.append(
            jnp.zeros((tenants, 2 * rank * piece), jnp.float32)
            .at[owners]
            .add(recv_in[:, local].reshape(dp_size * ex_size, -1))
        )
        sums_down.append(
            jnp.zeros((tenants, rank * piece), jnp.float32)
            .at[owners]
            .add(recv_down[:, local].reshape(dp_size * ex_size, -1))
        )
    grad_in = jnp.stack(sums_in, axis=0).reshape(exp_dev, tenants, 2 * rank, piece)
    grad_down = jnp.stack(sums_down, axis=0).reshape(exp_dev, tenants, rank, piece)
    return (adapted, grad_tokens, grad_weight, grad_in, grad_down)


def shards(*arrays):
    rank, piece = arrays[6].shape[2:]
    whole_tiles = piece % 128 == 0 and rank % 16 == 0
    even = lax.axis_size("tensor") == 2 and lax.axis_size("dp") % 2 == 0
    return paged(*arrays) if whole_tiles and even else routed(*arrays)


def solution(mesh):
    return jax.shard_map(
        shards,
        mesh=mesh,
        in_specs=(
            P(("groups", "dp", "expert"), "tensor"),
            P(("groups", "dp", "expert"), None),
            P(("groups", "dp", "expert"), None),
            P("groups"),
            P(),
            P("expert", None, None, ("tensor", "dp")),
            P("expert", None, None, ("tensor", "dp")),
            P(("groups", "dp", "expert"), "tensor"),
        ),
        out_specs=(
            P(("groups", "dp", "expert"), "tensor"),
            P(("groups", "dp", "expert"), "tensor"),
            P(("groups", "dp", "expert"), None),
            P(("groups", "expert"), None, None, ("tensor", "dp")),
            P(("groups", "expert"), None, None, ("tensor", "dp")),
        ),
        check_vma=False,
    )
```
